256 devices in a mesh: grp: 4 (over y), dev: 64 (over x, z, core).
Axes of the slice: x: 4, y: 4, z: 8, core: 2. Of those that a mesh axis runs over, the one named last changes fastest.
Arguments:
- embeds: bfloat16 [524288, 512], P(('grp', 'dev')), may hold values from -6 to 6
- cluster: int32 [524288, 1], P(('grp', 'dev')), may hold values from 0 to 511; in each aligned block of 2048 rows (0 to 2047, 2048 to 4095, ...) at most 6 rows name the same one
Outputs:
- nearest: float32 [524288], P(('grp', 'dev'))
The draws below stay inside these ranges and needn't reach their ends.
Inputs may be any that keep to these rules, and one draw needn't show every extreme that they name: The rows of one device name any one cluster at most 6 times, a bound that some block reaches.
All inputs are finite; a program needn't handle non-finite values.
Results may differ from the reference program's by a relative error of at most 0.0013.
Values may be sent and summed in bfloat16 or wider, within the bound.
A program may use at most 64 MiB of HBM per device.

```python
import math
import jax
import jax.numpy as jnp
import numpy as np
from jax import lax

D = 512
ROWS_DEV = 2048
CL_DEV = 2
CAP = 6
CLUSTERS = 512
ROWS = 524288
N_GRP = 4
N_DEV = 64


def block_levels(rng, dims, split, least, high):
    loudness = 1.0
    for dim, parts in split:
        heights = jax.random.uniform(jax.random.fold_in(jax.random.fold_in(rng, 6), dim), (parts,), jnp.float32, least / len(split), high / len(split))
        loudness = loudness * jnp.repeat(jnp.exp(heights), dims[dim] // parts).reshape((-1,) + (1,) * (len(dims) - 1 - dim))
    return loudness


def deal_out(key, own, number, rows, amount, top, limit, lean):
    order = jax.random.permutation(key, amount)
    crowded, ordinary = shares(amount, rows * top, limit, lean, True), shares(amount, rows * top, limit, lean, False)
    places = jnp.arange(amount)

    def named(tallies, rotation):
        used = int((tallies > 0).sum())
        fixed = max(1, used // 4)
        moved = fixed + (places - fixed + rotation * (used - fixed)) % max(1, amount - fixed)
        return jnp.zeros((amount,), jnp.int32).at[order[jnp.where(places < fixed, places, moved)]].set(jnp.asarray(tallies, jnp.int32))

    tallies = jnp.where(number % 4 == 0, named(crowded, number // 4), named(ordinary, number - number // 4 - 1))
    mixed = jax.random.permutation(jax.random.fold_in(own, 3), amount)
    giver, receiver = mixed[0:amount // 2 * 2:2], mixed[1:amount // 2 * 2:2]
    margin = jnp.minimum(tallies[giver] - 1, limit - tallies[receiver]) // 2
    margin = jnp.where((giver == order[0]) | (receiver == order[0]) | (tallies[receiver] == 0), 0, jnp.maximum(margin, 0))
    moved = jax.random.randint(jax.random.fold_in(own, 4), (amount // 2,), 0, 1 << 20) % (margin + 1)
    tallies = tallies.at[giver].add(-moved).at[receiver].add(moved)
    members = jnp.searchsorted(jnp.cumsum(tallies), jnp.arange(rows * top), side="right").astype(jnp.int32)
    grid = members.reshape(top, rows).T
    grid = grid[jax.random.permutation(jax.random.fold_in(own, 1), rows)]
    rotation = jax.random.randint(jax.random.fold_in(own, 2), (rows, 1), 0, top)
    return jnp.take_along_axis(grid, (jnp.arange(top)[None, :] + rotation) % top, axis=1)


def shares(amount, total, limit, lean, full):
    loads = [(1 << 20) // math.isqrt(grade ** lean) + 1 for grade in range(1, amount + 1)]
    largest = limit if full else min(limit, max(-(-total // amount), total * loads[0] // sum(loads)))
    least = 1 if total - largest >= amount - 1 else 0
    holding, spare = [largest] + [least] * (amount - 1), total - largest - least * (amount - 1)
    while spare > 0:
        candidates = [i for i in range(1, amount) if holding[i] < largest] or [i for i in range(1, amount) if holding[i] < limit]
        whole, remaining = sum([loads[i] for i in candidates]), spare
        for i in candidates:
            addition = min(limit - holding[i], max(1, remaining * loads[i] // whole), spare)
            holding[i] = holding[i] + addition
            spare = spare - addition
    return np.array(holding)


def noise(rng, dims, deviation, reach, cuts=(), held_as=jnp.bfloat16):
    result = jax.random.normal(rng, dims, jnp.float32) * deviation
    if len(cuts) > 0:
        result = block_levels(rng, dims, cuts, -0.22, 0.18) * result
    return jnp.clip(result, min=-reach, max=reach).astype(held_as)


def setup_inputs(seed: int = 0) -> dict:
    seeds = jax.random.split(jax.random.key(seed), 3)
    embeds = noise(seeds[0], (ROWS, D), 1.0, 6.0, ((0, 256),))
    cluster_keys = jax.random.split(jax.random.fold_in(seeds[1], 1), ROWS // ROWS_DEV)
    cluster_turns = jax.random.permutation(jax.random.fold_in(seeds[1], 3), ROWS // ROWS_DEV)
    cluster = jax.vmap(lambda own, number: deal_out(jax.random.fold_in(seeds[1], 2), own, number, ROWS_DEV, CLUSTERS, 1, CAP, 2))(cluster_keys, cluster_turns).reshape((ROWS, 1))
    return {"embeds": embeds, "cluster": cluster}


def reference(embeds, cluster):
    floats = embeds.astype(jnp.float32)
    unit_rows = (floats * lax.rsqrt(lax.optimization_barrier(jnp.sum(floats * floats, axis=1, keepdims=True)) + 1e-06)).astype(jnp.bfloat16)
    cluster_ids = cluster[:, 0].astype(jnp.int32)
    sort_order = jnp.argsort(cluster_ids, stable=True).astype(jnp.int32)
    sorted_ids = cluster_ids[sort_order]
    longest = N_GRP * N_DEV * CAP
    total_clusters = N_GRP * N_DEV * CL_DEV
    counts = jax.ops.segment_sum(jnp.ones_like(cluster_ids), cluster_ids, num_segments=total_clusters).astype(jnp.int32)
    offsets = (jnp.cumsum(counts) - counts).astype(jnp.int32)
    sorted_rows = unit_rows[sort_order].astype(jnp.float32)
    padded = jnp.concatenate([sorted_rows, jnp.zeros((longest, D), jnp.float32)], axis=0)
    positions = jnp.arange(longest, dtype=jnp.int32)

    def per_cluster(index):
        first_row = offsets[index]
        size_here = counts[index]
        member_rows = lax.dynamic_slice(padded, (first_row, jnp.int32(0)), (longest, D))
        sims = jnp.dot(member_rows, member_rows.T, precision=lax.Precision.HIGHEST)
        keep_pair = (positions[:, None] < size_here) & (positions[None, :] < size_here) & (positions[:, None] != positions[None, :])
        return lax.optimization_barrier(jnp.max(jnp.where(keep_pair, sims, jnp.float32(-1.0)), axis=1))
    per_slot = lax.map(per_cluster, jnp.arange(total_clusters, dtype=jnp.int32))
    local_pos = jnp.arange(ROWS, dtype=jnp.int32) - offsets[sorted_ids]
    sorted_best = per_slot[sorted_ids, local_pos]
    return jnp.zeros((ROWS,), jnp.float32).at[sort_order].set(sorted_best)
```

```python
import functools

import jax
import jax.numpy as jnp
from jax import lax
from jax.experimental import pallas as pl
from jax.experimental.pallas import tpu as pltpu
from jax.sharding import PartitionSpec as P

LOGICAL = pl.DeviceIdType.LOGICAL
NY, NX, NZ, NC = 4, 4, 8, 2
N_DEV = NY * NX * NZ * NC
ROWS, FEAT = 2048, 512
OWN, CAP = 2, 6
N_CL = OWN * N_DEV
GROUP = NZ * NC
CHUNKS = N_DEV // GROUP
SLOTS = GROUP * CAP
STRIDE = 128
MSG_R, MSG_C = 16, 384
HEAD = 384
DEAD = 4.0
FAR = -1e6


def iota(shape, dim):
    return lax.broadcasted_iota(jnp.int32, shape, dim)


def ones_at(mask):
    return jnp.where(mask, 1.0, 0.0).astype(jnp.bfloat16)


def dot(a, b):
    return jnp.dot(a, b, preferred_element_type=jnp.float32)


def dot_t(a, b):
    return lax.dot_general(a, b, (((1,), (1,)), ((), ())), preferred_element_type=jnp.float32)


def split3(v):
    hi = v.astype(jnp.bfloat16)
    rest = v - hi.astype(jnp.float32)
    mid = rest.astype(jnp.bfloat16)
    lo = (rest - mid.astype(jnp.float32)).astype(jnp.bfloat16)
    return hi, mid, lo


def kernel(
    ids_ref, embeds_hbm, out_ref,
    embeds, send, recv, unit, bias, best, rank, place, pick,
    pack, unpack, ret_out, ret_in,
    load_sem, sent_sem, got_sem, in_sem, back_sent_sem, back_got_sem,
):
    my_y = lax.axis_index("grp")
    my_dev = lax.axis_index("dev")
    my_x = my_dev // (NZ * NC)
    my_z = (my_dev // NC) % NZ
    my_c = my_dev % NC

    load = pltpu.make_async_copy(embeds_hbm, embeds, load_sem)
    load.start()

    def plane(sign):
        return [
            (my_z + sign * (j % NZ) + NZ) % NZ * NC + (my_c + j // NZ) % NC for j in range(GROUP)
        ]

    def column(g, sign):
        y = (my_y + sign * (g // NX) + NY) % NY
        x = (my_x + sign * (g % NX) + NX) % NX
        return (y * NX + x) * (NZ * NC)

    near = plane(1)
    here = column(0, 1)

    barrier = pltpu.get_barrier_semaphore()
    for j in range(1, GROUP):
        pl.semaphore_signal(barrier, inc=1, device_id=here + near[j], device_id_type=LOGICAL)
    for g in range(1, CHUNKS):
        pl.semaphore_signal(
            barrier, inc=1, device_id=column(g, 1) + near[0], device_id_type=LOGICAL
        )

    tri = ones_at(
        (iota((128, 256), 0) < iota((128, 256), 1)) | (iota((128, 256), 1) >= 128)
    )

    def rank_block(b, seen):
        at = pl.ds(pl.multiple_of(b * 128, 128), 128)
        member = iota((N_CL, 128), 0) == ids_ref[:, at]
        sums = dot(ones_at(member), tri)
        rank[:, at] = jnp.sum(
            jnp.where(member, sums[:, :128] + seen, 0.0), axis=0, keepdims=True
        )
        return seen + sums[:, 128:]

    lax.fori_loop(0, ROWS // 128, rank_block, jnp.zeros((N_CL, 128), jnp.float32))

    ids = ids_ref[...]
    ranks = rank[...].astype(jnp.int32)
    owner = ids >> 1
    sub = ids & 1
    dy = ((owner >> 6) - my_y) & (NY - 1)
    dx = ((owner >> 4) - my_x) & (NX - 1)
    dz = ((owner >> 1) - my_z) & (NZ - 1)
    dc = (owner - my_c) & (NC - 1)
    chunk = dy * NX + dx
    member_of = dc * NZ + dz
    slot = sub * SLOTS + member_of * CAP + ranks
    place[...] = chunk * (OWN * SLOTS) + slot

    def block_matrix(rows, slots_dim, which):
        block = iota(rows, 1 - slots_dim)
        s = iota(rows, slots_dim)
        peer = block // MSG_R
        i = block % MSG_R
        if which == 0:
            q, ok = i, i < OWN * CAP
        else:
            q, ok = 3 * (i - OWN * CAP) + (which - 1), i >= OWN * CAP
        return peer, q, ok, s

    for which in range(4):
        peer, q, ok, s = block_matrix((GROUP * MSG_R, OWN * SLOTS), 1, which)
        pack[which] = ones_at(ok & (s == (q // CAP) * SLOTS + peer * CAP + q % CAP))
        peer, q, ok, s = block_matrix((OWN * STRIDE, GROUP * MSG_R), 0, which)
        unpack[which] = ones_at(ok & (s == (q // CAP) * STRIDE + peer * CAP + q % CAP))

    pl.semaphore_wait(barrier, GROUP - 1 + CHUNKS - 1)
    for g in range(1, CHUNKS):
        pl.semaphore_signal(in_sem, inc=1, device_id=column(g, 1) + near[0], device_id_type=LOGICAL)
    pl.semaphore_wait(in_sem, CHUNKS - 1)
    load.wait()

    def make_chunk(g):
        hit = iota((OWN * SLOTS, ROWS), 0) == place[...] - g * (OWN * SLOTS)
        chosen = jnp.where(hit, 1.0, 0.0)
        live = jnp.sum(chosen, axis=1, keepdims=True)
        rows = dot(chosen.astype(jnp.bfloat16), embeds[...])
        rows = rows * lax.rsqrt(jnp.sum(rows * rows, axis=1, keepdims=True) + 1e-06)
        first = (iota((OWN * SLOTS, FEAT), 1) == 0) & (live < 0.5)
        rows = jnp.where(first, DEAD, rows).astype(jnp.bfloat16)
        tail = rows[:, HEAD:]
        for c in range(3):
            lanes = slice(c * 128, (c + 1) * 128)
            block = dot(pack[0], rows[:, lanes]) + dot(pack[1 + c], tail)
            send[pl.ds(g * GROUP, GROUP), :, lanes] = block.astype(jnp.bfloat16).reshape(
                GROUP, MSG_R, 128
            )

    def send_chunk(g, first):
        base = column(g, 1)
        for j in range(first, GROUP):
            k = g * GROUP + j
            pltpu.make_async_remote_copy(
                src_ref=send.at[k], dst_ref=recv.at[k], send_sem=sent_sem, recv_sem=got_sem.at[g],
                device_id=base + near[j], device_id_type=LOGICAL,
            ).start()

    make_chunk(0)
    send_chunk(0, 1)
    pltpu.make_async_copy(send.at[0], recv.at[0], got_sem.at[0]).start()

    def send_step(g, carry):
        make_chunk(g)
        send_chunk(g, 0)
        return carry

    lax.fori_loop(1, CHUNKS, send_step, 0)

    for s in range(OWN):
        unit[s] = jnp.zeros((CHUNKS * STRIDE, FEAT), jnp.bfloat16)
        bias[s] = jnp.full((CHUNKS * STRIDE, 128), FAR, jnp.float32)
        best[s] = jnp.full((1, CHUNKS * STRIDE), -1.0, jnp.float32)
    pick[...] = ones_at(iota((N_DEV, ROWS), 0) == chunk * GROUP + member_of)

    def got_step(g, carry):
        mine = pl.ds(g * GROUP, GROUP)
        pltpu.make_async_copy(recv.at[mine], recv.at[mine], got_sem.at[g]).wait()
        block = recv[mine].reshape(GROUP * MSG_R, MSG_C)
        head = dot(unpack[0], block)
        tail = (
            dot(unpack[1], block[:, :128])
            + dot(unpack[2], block[:, 128:256])
            + dot(unpack[3], block[:, 256:])
        )
        at = pl.ds(pl.multiple_of(g * STRIDE, STRIDE), STRIDE)
        for s in range(OWN):
            part = slice(s * STRIDE, (s + 1) * STRIDE)
            new = jnp.concatenate([head[part], tail[part]], axis=1).astype(jnp.bfloat16)
            empty = (head[part, :1] > 2.0) | (iota((STRIDE, 1), 0) >= SLOTS)
            new_bias = jnp.where(empty, FAR, 0.0)
            held = unit[s]
            by_old = jnp.max(dot_t(held, new) + bias[s], axis=0, keepdims=True)
            by_new = jnp.max(dot_t(new, held) + new_bias, axis=0, keepdims=True)
            among = dot_t(new, new) + new_bias
            among = jnp.where(
                iota((STRIDE, STRIDE), 0) == iota((STRIDE, STRIDE), 1), -1.0, among
            )
            arrived = iota((1, CHUNKS * STRIDE), 1) < g * STRIDE
            best[s] = jnp.maximum(best[s], jnp.where(arrived, by_new, -1.0))
            best[s, :, at] = jnp.maximum(
                jnp.maximum(by_old, jnp.max(among, axis=0, keepdims=True)), -1.0
            )
            unit[s, at] = new
            bias[s, at] = jnp.broadcast_to(new_bias, (STRIDE, 128))
        return carry

    lax.fori_loop(0, CHUNKS, got_step, 0)

    far = plane(-1)
    for s in range(OWN):
        for g in range(CHUNKS):
            ret_out[g, s : s + 1] = best[s, :, g * STRIDE : (g + 1) * STRIDE]

    def return_chunk(g, first):
        base = column(g, -1)
        for j in range(first, GROUP):
            pltpu.make_async_remote_copy(
                src_ref=ret_out.at[g], dst_ref=ret_in.at[g * GROUP + j],
                send_sem=back_sent_sem, recv_sem=back_got_sem,
                device_id=base + far[j], device_id_type=LOGICAL,
            ).start()

    pltpu.make_async_copy(ret_out.at[0], ret_in.at[0], back_got_sem).start()
    return_chunk(0, 1)

    def return_step(g, carry):
        return_chunk(g, 0)
        return carry

    lax.fori_loop(1, CHUNKS, return_step, 0)
    pltpu.make_async_copy(ret_in, ret_in, back_got_sem).wait()

    wanted = (iota((N_DEV, 128), 1) // CAP) == (iota((N_DEV, 128), 0) % GROUP)
    wanted &= iota((N_DEV, 128), 1) < SLOTS
    answers = []
    by_rank = ones_at(
        (iota((8, 128), 1) % CAP == iota((8, 128), 0)) & (iota((8, 128), 1) < SLOTS)
    )
    for s in range(OWN):
        values = jnp.where(wanted, ret_in[:, s, :], 0.0)
        hi, mid, lo = split3(values)
        answers.append(dot_t(by_rank, hi) + dot_t(by_rank, mid) + dot_t(by_rank, lo))
    answers = jnp.concatenate(answers, axis=0)
    hi, mid, lo = split3(answers)
    spread = dot(hi, pick[...]) + dot(mid, pick[...]) + dot(lo, pick[...])
    ids = ids_ref[...]
    row = (ids & 1) * 8 + rank[...].astype(jnp.int32)
    out_ref[...] = jnp.sum(
        jnp.where(iota((16, ROWS), 0) == row, spread, 0.0), axis=0, keepdims=True
    )

    others = pl.ds(0, N_DEV - 1)
    pltpu.make_async_copy(send.at[others], send.at[others], sent_sem).wait()
    pltpu.make_async_copy(ret_in.at[others], ret_in.at[others], back_sent_sem).wait()


def on_device(embeds, cluster):
    nearest = pl.pallas_call(
        kernel,
        out_shape=jax.ShapeDtypeStruct((1, ROWS), jnp.float32),
        in_specs=[
            pl.BlockSpec(memory_space=pltpu.VMEM),
            pl.BlockSpec(memory_space=pl.ANY),
        ],
        out_specs=pl.BlockSpec(memory_space=pltpu.VMEM),
        scratch_shapes=[
            pltpu.VMEM((ROWS, FEAT), jnp.bfloat16),
            pltpu.VMEM((N_DEV, MSG_R, MSG_C), jnp.bfloat16),
            pltpu.VMEM((N_DEV, MSG_R, MSG_C), jnp.bfloat16),
            pltpu.VMEM((OWN, CHUNKS * STRIDE, FEAT), jnp.bfloat16),
            pltpu.VMEM((OWN, CHUNKS * STRIDE, 128), jnp.float32),
            pltpu.VMEM((OWN, 1, CHUNKS * STRIDE), jnp.float32),
            pltpu.VMEM((1, ROWS), jnp.float32),
            pltpu.VMEM((1, ROWS), jnp.int32),
            pltpu.VMEM((N_DEV, ROWS), jnp.bfloat16),
            pltpu.VMEM((4, GROUP * MSG_R, OWN * SLOTS), jnp.bfloat16),
            pltpu.VMEM((4, OWN * STRIDE, GROUP * MSG_R), jnp.bfloat16),
            pltpu.VMEM((CHUNKS, OWN, 128), jnp.float32),
            pltpu.VMEM((N_DEV, OWN, 128), jnp.float32),
            pltpu.SemaphoreType.DMA,
            pltpu.SemaphoreType.DMA,
            pltpu.SemaphoreType.DMA((CHUNKS,)),
            pltpu.SemaphoreType.REGULAR,
            pltpu.SemaphoreType.DMA,
            pltpu.SemaphoreType.DMA,
        ],
        compiler_params=pltpu.CompilerParams(
            collective_id=0, has_side_effects=True, vmem_limit_bytes=48 * 1024 * 1024
        ),
    )(cluster.reshape(1, ROWS), embeds)
    return nearest.reshape(ROWS)


def solution(mesh):
    return jax.shard_map(
        on_device,
        mesh=mesh,
        in_specs=(P(("grp", "dev"), None), P(("grp", "dev"), None)),
        out_specs=P(("grp", "dev")),
        check_vma=False,
    )
```

```python
import functools

import jax
import jax.numpy as jnp
from jax import lax
from jax.experimental import pallas as pl
from jax.experimental.pallas import tpu as pltpu
from jax.sharding import PartitionSpec as P

LOGICAL = pl.DeviceIdType.LOGICAL
NY, NX, NZ, NC = 4, 4, 8, 2
N_DEV = NY * NX * NZ * NC
ROWS, FEAT = 2048, 512
OWN, CAP = 2, 6
N_CL = OWN * N_DEV
GROUP = NZ * NC
CHUNKS = N_DEV // GROUP
SLOTS = GROUP * CAP
STRIDE = 128
HALF = NZ * CAP
MSG_R, MSG_C = 16, 384
HEAD = 384
DEAD = 4.0
FAR = -1e6


def iota(shape, dim):
    return lax.broadcasted_iota(jnp.int32, shape, dim)


def ones_at(mask):
    return jnp.where(mask, 1.0, 0.0).astype(jnp.bfloat16)


def dot(a, b):
    return jnp.dot(a, b, preferred_element_type=jnp.float32)


def dot_t(a, b):
    return lax.dot_general(a, b, (((1,), (1,)), ((), ())), preferred_element_type=jnp.float32)


def split3(v):
    hi = v.astype(jnp.bfloat16)
    rest = v - hi.astype(jnp.float32)
    mid = rest.astype(jnp.bfloat16)
    lo = (rest - mid.astype(jnp.float32)).astype(jnp.bfloat16)
    return hi, mid, lo


def kernel(
    ids_ref, embeds_hbm, out_ref,
    embeds, send, recv, unit, bias, best, rank, pick,
    pack, unpack, tri, wanted, back_out, back_mid, back_half, back_in,
    load_sem, sent_sem, got_sem, in_sem, back_sent_sem, back_got_sem,
):
    my_y = lax.axis_index("grp")
    my_dev = lax.axis_index("dev")
    my_x = my_dev // (NZ * NC)
    my_z = (my_dev // NC) % NZ
    my_c = my_dev % NC

    load = pltpu.make_async_copy(embeds_hbm, embeds, load_sem)
    load.start()

    def plane(sign):
        return [
            (my_z + sign * (j % NZ) + NZ) % NZ * NC + (my_c + j // NZ) % NC for j in range(GROUP)
        ]

    def column(g, sign):
        y = (my_y + sign * (g // NX) + NY) % NY
        x = (my_x + sign * (g % NX) + NX) % NX
        return (y * NX + x) * (NZ * NC)

    near = plane(1)
    here = column(0, 1)

    barrier = pltpu.get_barrier_semaphore()
    for j in range(1, GROUP):
        pl.semaphore_signal(barrier, inc=1, device_id=here + near[j], device_id_type=LOGICAL)
    for g in range(1, CHUNKS):
        pl.semaphore_signal(
            barrier, inc=1, device_id=column(g, 1) + near[0], device_id_type=LOGICAL
        )

    tri[...] = ones_at(
        (iota((128, 256), 0) < iota((128, 256), 1)) | (iota((128, 256), 1) >= 128)
    )

    ids = ids_ref[...]
    owner = ids >> 1
    sub = ids & 1
    dy = ((owner >> 6) - my_y) & (NY - 1)
    dx = ((owner >> 4) - my_x) & (NX - 1)
    dz = ((owner >> 1) - my_z) & (NZ - 1)
    dc = (owner - my_c) & (NC - 1)
    chunk = dy * NX + dx
    member_of = dc * NZ + dz
    rank[...] = jnp.zeros((1, ROWS), jnp.int32)

    def block_matrix(rows, slots_dim, which):
        block = iota(rows, 1 - slots_dim)
        s = iota(rows, slots_dim)
        peer = block // MSG_R
        i = block % MSG_R
        if which == 0:
            q, ok = i, i < OWN * CAP
        else:
            q, ok = 3 * (i - OWN * CAP) + (which - 1), i >= OWN * CAP
        return peer, q, ok, s

    for which in range(4):
        peer, q, ok, s = block_matrix((GROUP * MSG_R, OWN * SLOTS), 1, which)
        pack[which] = ones_at(ok & (s == (q // CAP) * SLOTS + peer * CAP + q % CAP))

    def make_chunk(g):
        mine = chunk == g
        member = iota((OWN * GROUP, ROWS), 0) == jnp.where(mine, sub * GROUP + member_of, -1)
        blocks = [slice(b * 128, (b + 1) * 128) for b in range(ROWS // 128)]
        flags = ones_at(member)
        sums = dot(jnp.concatenate([flags[:, b] for b in blocks], axis=0), tri[...])
        seen = jnp.zeros((OWN * GROUP, 128), jnp.float32)
        ranks = []
        for n, b in enumerate(blocks):
            part = sums[n * OWN * GROUP : (n + 1) * OWN * GROUP]
            ranks.append(
                jnp.sum(
                    jnp.where(member[:, b], part[:, :128] + seen, 0.0), axis=0, keepdims=True
                )
            )
            seen = seen + part[:, 128:]
        ranks = jnp.concatenate(ranks, axis=1).astype(jnp.int32)
        rank[...] += ranks
        place = jnp.where(mine, sub * SLOTS + member_of * CAP + ranks, -1)

        hit = iota((OWN * SLOTS, ROWS), 0) == place
        chosen = jnp.where(hit, 1.0, 0.0)
        live = jnp.sum(chosen, axis=1, keepdims=True)
        rows = dot(chosen.astype(jnp.bfloat16), embeds[...])
        rows = rows * lax.rsqrt(jnp.sum(rows * rows, axis=1, keepdims=True) + 1e-06)
        first = (iota((OWN * SLOTS, FEAT), 1) == 0) & (live < 0.5)
        rows = jnp.where(first, DEAD, rows).astype(jnp.bfloat16)
        tail = rows[:, HEAD:]
        for c in range(3):
            lanes = slice(c * 128, (c + 1) * 128)
            block = dot(pack[0], rows[:, lanes]) + dot(pack[1 + c], tail)
            send[pl.ds(g * GROUP, GROUP), :, lanes] = block.astype(jnp.bfloat16).reshape(
                GROUP, MSG_R, 128
            )

    def send_chunk(g, first):
        base = column(g, 1)
        for j in range(first, GROUP):
            k = g * GROUP + j
            pltpu.make_async_remote_copy(
                src_ref=send.at[k], dst_ref=recv.at[k], send_sem=sent_sem, recv_sem=got_sem.at[g],
                device_id=base + near[j], device_id_type=LOGICAL,
            ).start()

    pl.semaphore_wait(barrier, GROUP - 1 + CHUNKS - 1)
    for g in range(1, CHUNKS):
        pl.semaphore_signal(in_sem, inc=1, device_id=column(g, 1) + near[0], device_id_type=LOGICAL)
    load.wait()
    make_chunk(0)
    send_chunk(0, 1)
    pltpu.make_async_copy(send.at[0], recv.at[0], got_sem.at[0]).start()

    pl.semaphore_wait(in_sem, CHUNKS - 1)

    def send_step(g, carry):
        make_chunk(g)
        send_chunk(g, 0)
        return carry

    lax.fori_loop(1, CHUNKS, send_step, 0)

    for s in range(OWN):
        unit[s] = jnp.zeros((CHUNKS * STRIDE, FEAT), jnp.bfloat16)
        bias[s] = jnp.full((1, CHUNKS * STRIDE), FAR, jnp.float32)
        best[s] = jnp.full((1, CHUNKS * STRIDE), -1.0, jnp.float32)
    for which in range(4):
        peer, q, ok, s = block_matrix((OWN * STRIDE, GROUP * MSG_R), 0, which)
        unpack[which] = ones_at(ok & (s == (q // CAP) * STRIDE + peer * CAP + q % CAP))
    pick[...] = ones_at(iota((N_DEV, ROWS), 0) == member_of * CHUNKS + chunk)
    lane = iota((N_DEV, 128), 1)
    wanted[...] = jnp.where(
        ((lane % HALF) // CAP == (iota((N_DEV, 128), 0) // CHUNKS) % NZ) & (lane < OWN * HALF),
        1.0,
        0.0,
    )

    def got_step(g, carry):
        mine = pl.ds(g * GROUP, GROUP)
        pltpu.make_async_copy(recv.at[mine], recv.at[mine], got_sem.at[g]).wait()
        block = recv[mine].reshape(GROUP * MSG_R, MSG_C)
        head = dot(unpack[0], block)
        tail = (
            dot(unpack[1], block[:, :128])
            + dot(unpack[2], block[:, 128:256])
            + dot(unpack[3], block[:, 256:])
        )
        at = pl.ds(pl.multiple_of(g * STRIDE, STRIDE), STRIDE)
        for s in range(OWN):
            part = slice(s * STRIDE, (s + 1) * STRIDE)
            new = jnp.concatenate([head[part], tail[part]], axis=1).astype(jnp.bfloat16)
            empty = (head[part, :1] > 2.0) | (iota((STRIDE, 1), 0) >= SLOTS)
            new_bias = jnp.where(empty, FAR, 0.0)
            same = iota((STRIDE, STRIDE), 0) == iota((STRIDE, STRIDE), 1)
            new_row = jnp.sum(jnp.where(same, new_bias, 0.0), axis=0, keepdims=True)
            sims = dot_t(new, unit[s])
            by_new = jnp.max(sims + new_bias, axis=0, keepdims=True)
            by_old = jnp.full((STRIDE, STRIDE), -1.0, jnp.float32)
            for h in range(CHUNKS):
                lanes = slice(h * STRIDE, (h + 1) * STRIDE)
                by_old = jnp.maximum(by_old, sims[:, lanes] + bias[s, :, lanes])
            by_old = jnp.max(by_old.T, axis=0, keepdims=True)
            among = jnp.where(same, -1.0, dot_t(new, new) + new_bias)
            arrived = iota((1, CHUNKS * STRIDE), 1) < g * STRIDE
            best[s] = jnp.maximum(best[s], jnp.where(arrived, by_new, -1.0))
            best[s, :, at] = jnp.maximum(
                jnp.maximum(by_old, jnp.max(among, axis=0, keepdims=True)), -1.0
            )
            unit[s, at] = new
            bias[s, :, at] = new_row
        return carry

    lax.fori_loop(0, CHUNKS, got_step, 0)

    far = plane(-1)
    for s in range(OWN):
        for g in range(CHUNKS):
            back_out[g, s : s + 1] = best[s, :, g * STRIDE : (g + 1) * STRIDE]
    for g in range(1, CHUNKS):
        pltpu.make_async_remote_copy(
            src_ref=back_out.at[g], dst_ref=back_mid.at[g],
            send_sem=back_sent_sem.at[0], recv_sem=back_got_sem.at[0],
            device_id=column(g, -1) + far[0], device_id_type=LOGICAL,
        ).start()
    back_mid[0] = back_out[0]
    rest = pl.ds(1, CHUNKS - 1)
    pltpu.make_async_copy(back_mid.at[rest], back_mid.at[rest], back_got_sem.at[0]).wait()
    lane = iota((CHUNKS, 128), 1)
    first, second = back_mid[:, 0, :], back_mid[:, 1, :]
    back_half[0] = jnp.where(lane < HALF, first, pltpu.roll(second, HALF, 1))
    back_half[1] = jnp.where(lane < HALF, pltpu.roll(first, 128 - HALF, 1), second)
    for j in range(1, GROUP):
        pltpu.make_async_remote_copy(
            src_ref=back_half.at[j // NZ], dst_ref=back_in.at[j],
            send_sem=back_sent_sem.at[1], recv_sem=back_got_sem.at[1],
            device_id=here + far[j], device_id_type=LOGICAL,
        ).start()
    back_in[0] = back_half[0]
    rest = pl.ds(1, GROUP - 1)
    pltpu.make_async_copy(back_in.at[rest], back_in.at[rest], back_got_sem.at[1]).wait()

    at_row, at_lane = iota((16, 128), 0), iota((16, 128), 1)
    by_rank = ones_at(
        (at_lane < OWN * HALF) & (at_row == at_lane // HALF * 8 + at_lane % HALF % CAP)
    )
    values = jnp.where(wanted[...] > 0.5, back_in[...].reshape(N_DEV, 128), 0.0)
    hi, mid, lo = split3(values)
    answers = dot_t(by_rank, hi) + dot_t(by_rank, mid) + dot_t(by_rank, lo)
    hi, mid, lo = split3(answers)
    spread = dot(hi, pick[...]) + dot(mid, pick[...]) + dot(lo, pick[...])
    row = (ids_ref[...] & 1) * 8 + rank[...]
    out_ref[...] = jnp.sum(
        jnp.where(iota((16, ROWS), 0) == row, spread, 0.0), axis=0, keepdims=True
    )

    others = pl.ds(0, N_DEV - 1)
    pltpu.make_async_copy(send.at[others], send.at[others], sent_sem).wait()
    pltpu.make_async_copy(back_out.at[rest], back_out.at[rest], back_sent_sem.at[0]).wait()
    pltpu.make_async_copy(back_in.at[rest], back_in.at[rest], back_sent_sem.at[1]).wait()


def on_device(embeds, cluster):
    nearest = pl.pallas_call(
        kernel,
        out_shape=jax.ShapeDtypeStruct((1, ROWS), jnp.float32),
        in_specs=[
            pl.BlockSpec(memory_space=pltpu.VMEM),
            pl.BlockSpec(memory_space=pl.ANY),
        ],
        out_specs=pl.BlockSpec(memory_space=pltpu.VMEM),
        scratch_shapes=[
            pltpu.VMEM((ROWS, FEAT), jnp.bfloat16),
            pltpu.VMEM((N_DEV, MSG_R, MSG_C), jnp.bfloat16),
            pltpu.VMEM((N_DEV, MSG_R, MSG_C), jnp.bfloat16),
            pltpu.VMEM((OWN, CHUNKS * STRIDE, FEAT), jnp.bfloat16),
            pltpu.VMEM((OWN, 1, CHUNKS * STRIDE), jnp.float32),
            pltpu.VMEM((OWN, 1, CHUNKS * STRIDE), jnp.float32),
            pltpu.VMEM((1, ROWS), jnp.int32),
            pltpu.VMEM((N_DEV, ROWS), jnp.bfloat16),
            pltpu.VMEM((4, GROUP * MSG_R, OWN * SLOTS), jnp.bfloat16),
            pltpu.VMEM((4, OWN * STRIDE, GROUP * MSG_R), jnp.bfloat16),
            pltpu.VMEM((128, 256), jnp.bfloat16),
            pltpu.VMEM((N_DEV, 128), jnp.float32),
            pltpu.VMEM((CHUNKS, OWN, 128), jnp.float32),
            pltpu.VMEM((CHUNKS, OWN, 128), jnp.float32),
            pltpu.VMEM((NC, CHUNKS, 128), jnp.float32),
            pltpu.VMEM((GROUP, CHUNKS, 128), jnp.float32),
            pltpu.SemaphoreType.DMA,
            pltpu.SemaphoreType.DMA,
            pltpu.SemaphoreType.DMA((CHUNKS,)),
            pltpu.SemaphoreType.REGULAR,
            pltpu.SemaphoreType.DMA((2,)),
            pltpu.SemaphoreType.DMA((2,)),
        ],
        compiler_params=pltpu.CompilerParams(
            collective_id=0, has_side_effects=True, vmem_limit_bytes=48 * 1024 * 1024
        ),
    )(cluster.reshape(1, ROWS), embeds)
    return nearest.reshape(ROWS)


def solution(mesh):
    return jax.shard_map(
        on_device,
        mesh=mesh,
        in_specs=(P(("grp", "dev"), None), P(("grp", "dev"), None)),
        out_specs=P(("grp", "dev")),
        check_vma=False,
    )
```

```python
import functools

import jax
import jax.numpy as jnp
from jax import lax
from jax.experimental import pallas as pl
from jax.experimental.pallas import tpu as pltpu
from jax.sharding import PartitionSpec as P

LOGICAL = pl.DeviceIdType.LOGICAL
NY, NX, NZ, NC = 4, 4, 8, 2
N_DEV = NY * NX * NZ * NC
ROWS, FEAT = 2048, 512
OWN, CAP = 2, 6
N_CL = OWN * N_DEV
GROUP = NZ * NC
CHUNKS = N_DEV // GROUP
SLOTS = GROUP * CAP
STRIDE = 128
HALF = NZ * CAP
MSG_R, MSG_C = 16, 384
HEAD = 384
DEAD = 4.0
FAR = -1e6
DIRECT = 4
EXTRA = CAP - DIRECT
SPILL = 64
PAIR = 2 * GROUP
OWNERS = NY * NX * NC
D_STEPS = N_DEV // PAIR
E_STEPS = 4
EARLY = 1
Z_ORDER = (1, 7, 2, 6, 3, 5, 4)
AHEAD = 6
BEFORE = 5
E_OWN = OWNERS // E_STEPS
LANES = 128
WIDTH = (D_STEPS + E_STEPS) * LANES


def iota(shape, dim):
    return lax.broadcasted_iota(jnp.int32, shape, dim)


def ones_at(mask):
    return jnp.where(mask, 1.0, 0.0).astype(jnp.bfloat16)


def dot(a, b):
    return jnp.dot(a, b, preferred_element_type=jnp.float32)


def dot_t(a, b):
    return lax.dot_general(a, b, (((1,), (1,)), ((), ())), preferred_element_type=jnp.float32)


def split3(v):
    hi = v.astype(jnp.bfloat16)
    rest = v - hi.astype(jnp.float32)
    mid = rest.astype(jnp.bfloat16)
    lo = (rest - mid.astype(jnp.float32)).astype(jnp.bfloat16)
    return hi, mid, lo


def padded_kernel(
    ids_ref, embeds_hbm, out_ref,
    embeds, send, recv, unit, bias, best, rank, pick,
    pack, unpack, tri, wanted, back_out, back_mid, back_half, back_in,
    load_sem, sent_sem, got_sem, in_sem, back_sent_sem, back_got_sem,
):
    my_y = lax.axis_index("grp")
    my_dev = lax.axis_index("dev")
    my_x = my_dev // (NZ * NC)
    my_z = (my_dev // NC) % NZ
    my_c = my_dev % NC

    load = pltpu.make_async_copy(embeds_hbm, embeds, load_sem)
    load.start()

    def plane(sign):
        return [
            (my_z + sign * (j % NZ) + NZ) % NZ * NC + (my_c + j // NZ) % NC for j in range(GROUP)
        ]

    def column(g, sign):
        y = (my_y + sign * (g // NX) + NY) % NY
        x = (my_x + sign * (g % NX) + NX) % NX
        return (y * NX + x) * (NZ * NC)

    near = plane(1)
    here = column(0, 1)

    barrier = pltpu.get_barrier_semaphore()
    for j in range(1, GROUP):
        pl.semaphore_signal(barrier, inc=1, device_id=here + near[j], device_id_type=LOGICAL)
    for g in range(1, CHUNKS):
        pl.semaphore_signal(
            barrier, inc=1, device_id=column(g, 1) + near[0], device_id_type=LOGICAL
        )

    tri[...] = ones_at(
        (iota((128, 256), 0) < iota((128, 256), 1)) | (iota((128, 256), 1) >= 128)
    )

    ids = ids_ref[...]
    owner = ids >> 1
    sub = ids & 1
    dy = ((owner >> 6) - my_y) & (NY - 1)
    dx = ((owner >> 4) - my_x) & (NX - 1)
    dz = ((owner >> 1) - my_z) & (NZ - 1)
    dc = (owner - my_c) & (NC - 1)
    chunk = dy * NX + dx
    member_of = dc * NZ + dz
    rank[...] = jnp.zeros((1, ROWS), jnp.int32)

    def block_matrix(rows, slots_dim, which):
        block = iota(rows, 1 - slots_dim)
        s = iota(rows, slots_dim)
        peer = block // MSG_R
        i = block % MSG_R
        if which == 0:
            q, ok = i, i < OWN * CAP
        else:
            q, ok = 3 * (i - OWN * CAP) + (which - 1), i >= OWN * CAP
        return peer, q, ok, s

    for which in range(4):
        peer, q, ok, s = block_matrix((GROUP * MSG_R, OWN * SLOTS), 1, which)
        pack[which] = ones_at(ok & (s == (q // CAP) * SLOTS + peer * CAP + q % CAP))

    def make_chunk(g):
        mine = chunk == g
        member = iota((OWN * GROUP, ROWS), 0) == jnp.where(mine, sub * GROUP + member_of, -1)
        blocks = [slice(b * 128, (b + 1) * 128) for b in range(ROWS // 128)]
        flags = ones_at(member)
        sums = dot(jnp.concatenate([flags[:, b] for b in blocks], axis=0), tri[...])
        seen = jnp.zeros((OWN * GROUP, 128), jnp.float32)
        ranks = []
        for n, b in enumerate(blocks):
            part = sums[n * OWN * GROUP : (n + 1) * OWN * GROUP]
            ranks.append(
                jnp.sum(
                    jnp.where(member[:, b], part[:, :128] + seen, 0.0), axis=0, keepdims=True
                )
            )
            seen = seen + part[:, 128:]
        ranks = jnp.concatenate(ranks, axis=1).astype(jnp.int32)
        rank[...] += ranks
        place = jnp.where(mine, sub * SLOTS + member_of * CAP + ranks, -1)

        hit = iota((OWN * SLOTS, ROWS), 0) == place
        chosen = jnp.where(hit, 1.0, 0.0)
        live = jnp.sum(chosen, axis=1, keepdims=True)
        rows = dot(chosen.astype(jnp.bfloat16), embeds[...])
        rows = rows * lax.rsqrt(jnp.sum(rows * rows, axis=1, keepdims=True) + 1e-06)
        first = (iota((OWN * SLOTS, FEAT), 1) == 0) & (live < 0.5)
        rows = jnp.where(first, DEAD, rows).astype(jnp.bfloat16)
        tail = rows[:, HEAD:]
        for c in range(3):
            lanes = slice(c * 128, (c + 1) * 128)
            block = dot(pack[0], rows[:, lanes]) + dot(pack[1 + c], tail)
            send[pl.ds(g * GROUP, GROUP), :, lanes] = block.astype(jnp.bfloat16).reshape(
                GROUP, MSG_R, 128
            )

    def send_chunk(g, first):
        base = column(g, 1)
        for j in range(first, GROUP):
            k = g * GROUP + j
            pltpu.make_async_remote_copy(
                src_ref=send.at[k], dst_ref=recv.at[k], send_sem=sent_sem, recv_sem=got_sem.at[g],
                device_id=base + near[j], device_id_type=LOGICAL,
            ).start()

    pl.semaphore_wait(barrier, GROUP - 1 + CHUNKS - 1)
    for g in range(1, CHUNKS):
        pl.semaphore_signal(in_sem, inc=1, device_id=column(g, 1) + near[0], device_id_type=LOGICAL)
    load.wait()
    make_chunk(0)
    send_chunk(0, 1)
    pltpu.make_async_copy(send.at[0], recv.at[0], got_sem.at[0]).start()

    pl.semaphore_wait(in_sem, CHUNKS - 1)

    def send_step(g, carry):
        make_chunk(g)
        send_chunk(g, 0)
        return carry

    lax.fori_loop(1, CHUNKS, send_step, 0)

    for s in range(OWN):
        unit[s] = jnp.zeros((CHUNKS * STRIDE, FEAT), jnp.bfloat16)
        bias[s] = jnp.full((1, CHUNKS * STRIDE), FAR, jnp.float32)
        best[s] = jnp.full((1, CHUNKS * STRIDE), -1.0, jnp.float32)
    for which in range(4):
        peer, q, ok, s = block_matrix((OWN * STRIDE, GROUP * MSG_R), 0, which)
        unpack[which] = ones_at(ok & (s == (q // CAP) * STRIDE + peer * CAP + q % CAP))
    pick[...] = ones_at(iota((N_DEV, ROWS), 0) == member_of * CHUNKS + chunk)
    lane = iota((N_DEV, 128), 1)
    wanted[...] = jnp.where(
        ((lane % HALF) // CAP == (iota((N_DEV, 128), 0) // CHUNKS) % NZ) & (lane < OWN * HALF),
        1.0,
        0.0,
    )

    def got_step(g, carry):
        mine = pl.ds(g * GROUP, GROUP)
        pltpu.make_async_copy(recv.at[mine], recv.at[mine], got_sem.at[g]).wait()
        block = recv[mine].reshape(GROUP * MSG_R, MSG_C)
        head = dot(unpack[0], block)
        tail = (
            dot(unpack[1], block[:, :128])
            + dot(unpack[2], block[:, 128:256])
            + dot(unpack[3], block[:, 256:])
        )
        at = pl.ds(pl.multiple_of(g * STRIDE, STRIDE), STRIDE)
        for s in range(OWN):
            part = slice(s * STRIDE, (s + 1) * STRIDE)
            new = jnp.concatenate([head[part], tail[part]], axis=1).astype(jnp.bfloat16)
            empty = (head[part, :1] > 2.0) | (iota((STRIDE, 1), 0) >= SLOTS)
            new_bias = jnp.where(empty, FAR, 0.0)
            same = iota((STRIDE, STRIDE), 0) == iota((STRIDE, STRIDE), 1)
            new_row = jnp.sum(jnp.where(same, new_bias, 0.0), axis=0, keepdims=True)
            sims = dot_t(new, unit[s])
            by_new = jnp.max(sims + new_bias, axis=0, keepdims=True)
            by_old = jnp.full((STRIDE, STRIDE), -1.0, jnp.float32)
            for h in range(CHUNKS):
                lanes = slice(h * STRIDE, (h + 1) * STRIDE)
                by_old = jnp.maximum(by_old, sims[:, lanes] + bias[s, :, lanes])
            by_old = jnp.max(by_old.T, axis=0, keepdims=True)
            among = jnp.where(same, -1.0, dot_t(new, new) + new_bias)
            arrived = iota((1, CHUNKS * STRIDE), 1) < g * STRIDE
            best[s] = jnp.maximum(best[s], jnp.where(arrived, by_new, -1.0))
            best[s, :, at] = jnp.maximum(
                jnp.maximum(by_old, jnp.max(among, axis=0, keepdims=True)), -1.0
            )
            unit[s, at] = new
            bias[s, :, at] = new_row
        return carry

    lax.fori_loop(0, CHUNKS, got_step, 0)

    far = plane(-1)
    for s in range(OWN):
        for g in range(CHUNKS):
            back_out[g, s : s + 1] = best[s, :, g * STRIDE : (g + 1) * STRIDE]
    for g in range(1, CHUNKS):
        pltpu.make_async_remote_copy(
            src_ref=back_out.at[g], dst_ref=back_mid.at[g],
            send_sem=back_sent_sem.at[0], recv_sem=back_got_sem.at[0],
            device_id=column(g, -1) + far[0], device_id_type=LOGICAL,
        ).start()
    back_mid[0] = back_out[0]
    rest = pl.ds(1, CHUNKS - 1)
    pltpu.make_async_copy(back_mid.at[rest], back_mid.at[rest], back_got_sem.at[0]).wait()
    lane = iota((CHUNKS, 128), 1)
    first, second = back_mid[:, 0, :], back_mid[:, 1, :]
    back_half[0] = jnp.where(lane < HALF, first, pltpu.roll(second, HALF, 1))
    back_half[1] = jnp.where(lane < HALF, pltpu.roll(first, 128 - HALF, 1), second)
    for j in range(1, GROUP):
        pltpu.make_async_remote_copy(
            src_ref=back_half.at[j // NZ], dst_ref=back_in.at[j],
            send_sem=back_sent_sem.at[1], recv_sem=back_got_sem.at[1],
            device_id=here + far[j], device_id_type=LOGICAL,
        ).start()
    back_in[0] = back_half[0]
    rest = pl.ds(1, GROUP - 1)
    pltpu.make_async_copy(back_in.at[rest], back_in.at[rest], back_got_sem.at[1]).wait()

    at_row, at_lane = iota((16, 128), 0), iota((16, 128), 1)
    by_rank = ones_at(
        (at_lane < OWN * HALF) & (at_row == at_lane // HALF * 8 + at_lane % HALF % CAP)
    )
    values = jnp.where(wanted[...] > 0.5, back_in[...].reshape(N_DEV, 128), 0.0)
    hi, mid, lo = split3(values)
    answers = dot_t(by_rank, hi) + dot_t(by_rank, mid) + dot_t(by_rank, lo)
    hi, mid, lo = split3(answers)
    spread = dot(hi, pick[...]) + dot(mid, pick[...]) + dot(lo, pick[...])
    row = (ids_ref[...] & 1) * 8 + rank[...]
    out_ref[...] = jnp.sum(
        jnp.where(iota((16, ROWS), 0) == row, spread, 0.0), axis=0, keepdims=True
    )

    others = pl.ds(0, N_DEV - 1)
    pltpu.make_async_copy(send.at[others], send.at[others], sent_sem).wait()
    pltpu.make_async_copy(back_out.at[rest], back_out.at[rest], back_sent_sem.at[0]).wait()
    pltpu.make_async_copy(back_in.at[rest], back_in.at[rest], back_sent_sem.at[1]).wait()


def fast_kernel(
    ids_ref, embeds_hbm, out_ref, over_ref,
    embeds, send, recv, spill_out, spill_in, tag_out, tag_in, extra_out, extra_in,
    unit, bias, best, best_rows, rank, pick, undirect, unextra, tri, wanted,
    back_out, back_mid, back_half, back_in,
    load_sem, sent_sem, got_sem, in_sem, spill_sem, tag_sem, extra_sent_sem, extra_sem,
    back_sent_sem, back_got_sem,
):
    my_y = lax.axis_index("grp")
    my_dev = lax.axis_index("dev")
    my_x = my_dev // (NZ * NC)
    my_z = (my_dev // NC) % NZ
    my_c = my_dev % NC

    load = pltpu.make_async_copy(embeds_hbm, embeds, load_sem)
    load.start()

    def plane(sign):
        return [
            (my_z + sign * (j % NZ) + NZ) % NZ * NC + (my_c + j // NZ) % NC for j in range(GROUP)
        ]

    def column(g, sign):
        y = (my_y + sign * (g // NX) + NY) % NY
        x = (my_x + sign * (g % NX) + NX) % NX
        return (y * NX + x) * (NZ * NC)

    near = plane(1)
    here = column(0, 1)

    barrier = pltpu.get_barrier_semaphore()
    for j in range(1, GROUP):
        pl.semaphore_signal(barrier, inc=1, device_id=here + near[j], device_id_type=LOGICAL)
    for g in range(1, CHUNKS):
        pl.semaphore_signal(
            barrier, inc=1, device_id=column(g, 1) + near[0], device_id_type=LOGICAL
        )

    tri[...] = ones_at(
        (iota((128, 256), 0) < iota((128, 256), 1)) | (iota((128, 256), 1) >= 128)
    )

    ids = ids_ref[...]
    owner = ids >> 1
    sub = ids & 1
    dy = ((owner >> 6) - my_y) & (NY - 1)
    dx = ((owner >> 4) - my_x) & (NX - 1)
    dz = ((owner >> 1) - my_z) & (NZ - 1)
    dc = (owner - my_c) & (NC - 1)
    chunk = dy * NX + dx
    member_of = dc * NZ + dz
    rank[...] = jnp.zeros((1, ROWS), jnp.int32)

    def count_before(key, kinds):
        member = iota((kinds, ROWS), 0) == key
        blocks = [slice(b * 128, (b + 1) * 128) for b in range(ROWS // 128)]
        flags = ones_at(member)
        sums = dot(jnp.concatenate([flags[:, b] for b in blocks], axis=0), tri[...])
        seen = jnp.zeros((kinds, 128), jnp.float32)
        before = []
        for n, b in enumerate(blocks):
            part = sums[n * kinds : (n + 1) * kinds]
            before.append(
                jnp.sum(
                    jnp.where(member[:, b], part[:, :128] + seen, 0.0), axis=0, keepdims=True
                )
            )
            seen = seen + part[:, 128:]
        return jnp.concatenate(before, axis=1).astype(jnp.int32), seen

    def rank_chunk(g):
        key = jnp.where(chunk == g, sub * GROUP + member_of, -1)
        rank[...] += count_before(key, OWN * GROUP)[0]

    def chosen_rows(place, amount):
        chosen = jnp.where(iota((amount, ROWS), 0) == place, 1.0, 0.0)
        rows = dot(chosen.astype(jnp.bfloat16), embeds[...])
        rows = rows * lax.rsqrt(jnp.sum(rows * rows, axis=1, keepdims=True) + 1e-06)
        return chosen, rows

    def mark_empty(rows, chosen):
        empty = jnp.sum(chosen, axis=1, keepdims=True) < 0.5
        return jnp.where((iota(rows.shape, 1) == 0) & empty, DEAD, rows)

    def make_direct(first, chunks):
        order = chunk - first
        mine = (order >= 0) & (order < chunks) & (rank[...] < DIRECT)
        slot = ((order * GROUP + member_of) * OWN + sub) * DIRECT + rank[...]
        chosen, rows = chosen_rows(jnp.where(mine, slot, -1), chunks * GROUP * OWN * DIRECT)
        rows = mark_empty(rows, chosen).reshape(chunks * GROUP, OWN * DIRECT, FEAT)
        block = jnp.concatenate([rows[:, :, : FEAT // 2], rows[:, :, FEAT // 2 :]], axis=1)
        send[pl.ds(first * GROUP, chunks * GROUP)] = block.astype(jnp.bfloat16)

    def send_chunk(g, first, sem):
        base = column(g, 1)
        for j in range(first, GROUP):
            k = g * GROUP + j
            pltpu.make_async_remote_copy(
                src_ref=send.at[k], dst_ref=recv.at[k], send_sem=sent_sem, recv_sem=got_sem.at[sem],
                device_id=base + near[j], device_id_type=LOGICAL,
            ).start()

    rank_chunk(0)
    pl.semaphore_wait(barrier, GROUP - 1 + CHUNKS - 1)
    for g in range(1, CHUNKS):
        pl.semaphore_signal(in_sem, inc=1, device_id=column(g, 1) + near[0], device_id_type=LOGICAL)
    load.wait()
    make_direct(0, 1)
    send_chunk(0, 1, 0)
    pltpu.make_async_copy(send.at[0], recv.at[0], got_sem.at[0]).start()

    def rank_step(g, carry):
        rank_chunk(g)
        return carry

    def send_step(q, carry):
        make_direct(2 * q, 2)
        send_chunk(2 * q, 0, q)
        send_chunk(2 * q + 1, 0, q)
        return carry

    rank_chunk(1)
    pl.semaphore_wait(in_sem, CHUNKS - 1)
    make_direct(1, 1)
    send_chunk(1, 0, 0)

    def early_step(q, carry):
        rank_chunk(2 * q)
        rank_chunk(2 * q + 1)
        return send_step(q, carry)

    lax.fori_loop(1, EARLY, early_step, 0)
    lax.fori_loop(2 * EARLY, CHUNKS, rank_step, 0)

    beyond = rank[...] >= DIRECT
    spot, totals = count_before(jnp.where(beyond, dz, -1), 2 * NZ)
    over = jnp.max(totals, axis=(0, 1), keepdims=True) > SPILL
    over = jnp.where(over, 1.0, 0.0)
    place = jnp.where(beyond & (spot < SPILL), dz * SPILL + spot, -1)
    chosen, rows = chosen_rows(place, NZ * SPILL)
    spill_out[...] = rows.astype(jnp.bfloat16).reshape(NZ, SPILL, FEAT)
    spill_in[0] = rows[:SPILL].astype(jnp.bfloat16)
    label = ((chunk * NC + dc) * OWN + sub) * EXTRA + rank[...] - DIRECT + 1
    labels = jnp.sum(jnp.where(chosen > 0.5, label.astype(jnp.float32), 0.0), axis=1, keepdims=True)
    same = iota((LANES, LANES), 0) == iota((LANES, LANES), 1)
    for b in range(NZ * SPILL // LANES):
        part = labels[b * LANES : (b + 1) * LANES]
        line = jnp.sum(jnp.where(same, part, 0.0), axis=0, keepdims=True)
        tag_out[2 * b] = line.astype(jnp.int32)
        tag_out[2 * b + 1] = pltpu.roll(line, SPILL, 1).astype(jnp.int32)
    tag_in[0] = tag_out[0]
    for piece in range(SPILL // MSG_R):
        for d in Z_ORDER:
            rows = pl.ds(piece * MSG_R, MSG_R)
            pltpu.make_async_remote_copy(
                src_ref=spill_out.at[d, rows], dst_ref=spill_in.at[d, rows],
                send_sem=spill_sem.at[0], recv_sem=spill_sem.at[1],
                device_id=here + near[d], device_id_type=LOGICAL,
            ).start()
            if piece == 0:
                pltpu.make_async_remote_copy(
                    src_ref=tag_out.at[d], dst_ref=tag_in.at[d],
                    send_sem=tag_sem.at[0], recv_sem=tag_sem.at[1],
                    device_id=here + near[d], device_id_type=LOGICAL,
                ).start()

    lax.fori_loop(EARLY, AHEAD, send_step, 0)

    others = pl.ds(1, NZ - 1)
    pltpu.make_async_copy(spill_in.at[others], spill_in.at[others], spill_sem.at[1]).wait()
    pltpu.make_async_copy(tag_in.at[others], tag_in.at[others], tag_sem.at[1]).wait()
    lane = iota((1, LANES), 1)
    onward = []
    for b in range(NZ // 2):
        line = jnp.where(lane < SPILL, tag_in[2 * b], pltpu.roll(tag_in[2 * b + 1], SPILL, 1))
        at = line - 1
        at = (at >> 2) * (NZ * OWN * EXTRA) + (2 * b + (lane >> 6)) * (OWN * EXTRA) + (at & 3)
        onward.append(jnp.where(line > 0, at, -1))
    onward = jnp.concatenate(onward, axis=1)

    def onward_step(e, carry):
        amount = E_OWN * NZ * OWN * EXTRA
        chosen = jnp.where(iota((amount, NZ * SPILL), 0) + e * amount == onward, 1.0, 0.0)
        rows = dot(chosen.astype(jnp.bfloat16), spill_in[...].reshape(NZ * SPILL, FEAT))
        rows = mark_empty(rows, chosen).astype(jnp.bfloat16)
        extra_out[pl.ds(e * E_OWN, E_OWN)] = rows.reshape(E_OWN, NZ * OWN * EXTRA, FEAT)
        return carry

    lax.fori_loop(0, E_STEPS, onward_step, 0)
    pltpu.make_async_copy(extra_out.at[0], extra_in.at[0], extra_sem.at[0]).start()
    for j in range(E_OWN):
        for e in (1, 3, 2, 0):
            k = e * E_OWN + j
            if k > 0:
                pltpu.make_async_remote_copy(
                    src_ref=extra_out.at[k], dst_ref=extra_in.at[k],
                    send_sem=extra_sent_sem, recv_sem=extra_sem.at[e],
                    device_id=column(k // NC, 1) + near[j % NC * NZ], device_id_type=LOGICAL,
                ).start()

    lax.fori_loop(AHEAD, D_STEPS, send_step, 0)

    for s in range(OWN):
        unit[s] = jnp.zeros((WIDTH, FEAT), jnp.bfloat16)
        bias[s] = jnp.full((1, WIDTH), FAR, jnp.float32)
        best[s] = jnp.full((1, WIDTH), -1.0, jnp.float32)
    to, frm = iota((OWN * LANES, PAIR * MSG_R), 0), iota((OWN * LANES, PAIR * MSG_R), 1)
    slot = to % LANES
    at = slot // DIRECT * MSG_R + to // LANES * DIRECT + slot % DIRECT
    undirect[0] = ones_at(frm == at)
    undirect[1] = ones_at(frm == at + OWN * DIRECT)
    to, frm = iota((OWN * LANES, OWN * LANES), 0), iota((OWN * LANES, OWN * LANES), 1)
    slot = to % LANES
    unextra[...] = ones_at(
        frm == slot // EXTRA * (OWN * EXTRA) + to // LANES * EXTRA + slot % EXTRA
    )
    pick[...] = ones_at(iota((N_DEV, ROWS), 0) == member_of * CHUNKS + chunk)
    lane = iota((N_DEV, LANES), 1)
    lane_dz = jnp.where(lane < 64, lane % 32 // DIRECT, lane % 16 // EXTRA)
    wanted[...] = jnp.where(
        (lane_dz == (iota((N_DEV, LANES), 0) // CHUNKS) % NZ) & (lane < 96), 1.0, 0.0
    )

    def compare(t, both):
        at = pl.ds(pl.multiple_of(t * LANES, LANES), LANES)
        for s in range(OWN):
            part = both[s * LANES : (s + 1) * LANES]
            new = part.astype(jnp.bfloat16)
            new_bias = jnp.where(part[:, :1] > 2.0, FAR, 0.0)
            same = iota((LANES, LANES), 0) == iota((LANES, LANES), 1)
            new_row = jnp.sum(jnp.where(same, new_bias, 0.0), axis=0, keepdims=True)
            sims = dot_t(new, unit[s])
            by_new = jnp.max(sims + new_bias, axis=0, keepdims=True)
            by_old = jnp.full((LANES, LANES), -1.0, jnp.float32)
            for h in range(D_STEPS + E_STEPS):
                lanes = slice(h * LANES, (h + 1) * LANES)
                by_old = jnp.maximum(by_old, sims[:, lanes] + bias[s, :, lanes])
            by_old = jnp.max(by_old.T, axis=0, keepdims=True)
            among = jnp.where(same, -1.0, dot_t(new, new) + new_bias)
            best[s] = jnp.maximum(best[s], jnp.where(bias[s] > -1.0, by_new, -1.0))
            best[s, :, at] = jnp.maximum(
                jnp.maximum(by_old, jnp.max(among, axis=0, keepdims=True)), -1.0
            )
            unit[s, at] = new
            bias[s, :, at] = new_row

    def direct_step(q, carry):
        mine = pl.ds(q * PAIR, PAIR)
        pltpu.make_async_copy(recv.at[mine], recv.at[mine], got_sem.at[q]).wait()
        block = recv[mine].reshape(PAIR * MSG_R, FEAT // 2)
        compare(q, jnp.concatenate([dot(undirect[0], block), dot(undirect[1], block)], axis=1))
        return carry

    def extra_step(e, carry):
        mine = pl.ds(e * E_OWN, E_OWN)
        pltpu.make_async_copy(extra_in.at[mine], extra_in.at[mine], extra_sem.at[e]).wait()
        block = extra_in[mine].reshape(OWN * LANES, FEAT)
        compare(D_STEPS + e, dot(unextra[...], block))
        return carry

    lax.fori_loop(0, BEFORE, direct_step, 0)
    lax.fori_loop(0, E_STEPS, extra_step, 0)
    lax.fori_loop(BEFORE, D_STEPS, direct_step, 0)

    far = plane(-1)
    for s in range(OWN):
        for t in range(D_STEPS + E_STEPS):
            best_rows[s, t : t + 1] = best[s, :, t * LANES : (t + 1) * LANES]
    lane = iota((D_STEPS, LANES), 1)
    first, second = best_rows[0, :D_STEPS], best_rows[1, :D_STEPS]
    even = jnp.where(lane < 64, first, pltpu.roll(second, 64, 1))
    odd = jnp.where(lane < 64, pltpu.roll(first, 64, 1), second)
    for q in range(D_STEPS):
        back_out[2 * q, 0:1] = even[q : q + 1]
        back_out[2 * q + 1, 0:1] = odd[q : q + 1]
    first, second = best_rows[0, D_STEPS:], best_rows[1, D_STEPS:]
    for r in range(4):
        line = jnp.where(
            lane < 32,
            first if r == 0 else pltpu.roll(first, 128 - 32 * r, 1),
            second if r == 1 else pltpu.roll(second, (160 - 32 * r) % 128, 1),
        )
        line = jnp.where(lane < 96, line, over)
        for e in range(E_STEPS):
            back_out[4 * e + r, 1:2] = line[e : e + 1]
    for g in range(1, CHUNKS):
        pltpu.make_async_remote_copy(
            src_ref=back_out.at[g], dst_ref=back_mid.at[g],
            send_sem=back_sent_sem.at[0], recv_sem=back_got_sem.at[0],
            device_id=column(g, -1) + far[0], device_id_type=LOGICAL,
        ).start()
    back_mid[0] = back_out[0]
    rest = pl.ds(1, CHUNKS - 1)
    pltpu.make_async_copy(back_mid.at[rest], back_mid.at[rest], back_got_sem.at[0]).wait()
    lane = iota((CHUNKS, LANES), 1)
    main, more = back_mid[:, 0, :], back_mid[:, 1, :]
    over = jnp.max(jnp.where(lane < 96, 0.0, more), axis=(0, 1), keepdims=True)
    for h in range(NC):
        line = jnp.where(lane < 96, pltpu.roll(more, 48 - 16 * h, 1), over)
        line = jnp.where(lane < 80, pltpu.roll(more, 64 - 16 * h, 1), line)
        line = jnp.where(lane < 64, pltpu.roll(main, 96 - 32 * h, 1), line)
        back_half[h] = jnp.where(lane < 32, main if h == 0 else pltpu.roll(main, 96, 1), line)
    for j in range(1, GROUP):
        pltpu.make_async_remote_copy(
            src_ref=back_half.at[j // NZ], dst_ref=back_in.at[j],
            send_sem=back_sent_sem.at[1], recv_sem=back_got_sem.at[1],
            device_id=here + far[j], device_id_type=LOGICAL,
        ).start()
    back_in[0] = back_half[0]
    rest = pl.ds(1, GROUP - 1)
    pltpu.make_async_copy(back_in.at[rest], back_in.at[rest], back_got_sem.at[1]).wait()

    at_row, lane = iota((16, LANES), 0), iota((16, LANES), 1)
    kind = jnp.where(
        lane < 64, lane // 32 * 8 + lane % DIRECT, (lane - 64) // 16 * 8 + DIRECT + lane % EXTRA
    )
    by_rank = ones_at((lane < 96) & (at_row == kind))
    everything = back_in[...].reshape(N_DEV, LANES)
    values = jnp.where(wanted[...] > 0.5, everything, 0.0)
    hi, mid, lo = split3(values)
    answers = dot_t(by_rank, hi) + dot_t(by_rank, mid) + dot_t(by_rank, lo)
    hi, mid, lo = split3(answers)
    spread = dot(hi, pick[...]) + dot(mid, pick[...]) + dot(lo, pick[...])
    row = (ids_ref[...] & 1) * 8 + rank[...]
    out_ref[...] = jnp.sum(
        jnp.where(iota((16, ROWS), 0) == row, spread, 0.0), axis=0, keepdims=True
    )
    lane = iota((N_DEV, LANES), 1)
    over = jnp.max(jnp.where(lane < 96, 0.0, everything), axis=(0, 1), keepdims=True)
    over_ref[...] = jnp.broadcast_to(over, (1, LANES))

    peers = pl.ds(1, N_DEV - 1)
    pltpu.make_async_copy(send.at[peers], send.at[peers], sent_sem).wait()
    pltpu.make_async_copy(spill_out.at[others], spill_out.at[others], spill_sem.at[0]).wait()
    pltpu.make_async_copy(tag_out.at[others], tag_out.at[others], tag_sem.at[0]).wait()
    peers = pl.ds(1, OWNERS - 1)
    pltpu.make_async_copy(extra_out.at[peers], extra_out.at[peers], extra_sent_sem).wait()
    pltpu.make_async_copy(back_out.at[rest], back_out.at[rest], back_sent_sem.at[0]).wait()
    pltpu.make_async_copy(back_in.at[rest], back_in.at[rest], back_sent_sem.at[1]).wait()


def fast_nearest(ids, embeds):
    bf16, f32, i32 = jnp.bfloat16, jnp.float32, jnp.int32
    return pl.pallas_call(
        fast_kernel,
        out_shape=(
            jax.ShapeDtypeStruct((1, ROWS), f32),
            jax.ShapeDtypeStruct((1, LANES), f32),
        ),
        in_specs=[
            pl.BlockSpec(memory_space=pltpu.VMEM),
            pl.BlockSpec(memory_space=pl.ANY),
        ],
        out_specs=(
            pl.BlockSpec(memory_space=pltpu.VMEM),
            pl.BlockSpec(memory_space=pltpu.VMEM),
        ),
        scratch_shapes=[
            pltpu.VMEM((ROWS, FEAT), bf16),
            pltpu.VMEM((N_DEV, MSG_R, FEAT // 2), bf16),
            pltpu.VMEM((N_DEV, MSG_R, FEAT // 2), bf16),
            pltpu.VMEM((NZ, SPILL, FEAT), bf16),
            pltpu.VMEM((NZ, SPILL, FEAT), bf16),
            pltpu.VMEM((NZ, 1, LANES), i32),
            pltpu.VMEM((NZ, 1, LANES), i32),
            pltpu.VMEM((OWNERS, NZ * OWN * EXTRA, FEAT), bf16),
            pltpu.VMEM((OWNERS, NZ * OWN * EXTRA, FEAT), bf16),
            pltpu.VMEM((OWN, WIDTH, FEAT), bf16),
            pltpu.VMEM((OWN, 1, WIDTH), f32),
            pltpu.VMEM((OWN, 1, WIDTH), f32),
            pltpu.VMEM((OWN, 2 * D_STEPS, LANES), f32),
            pltpu.VMEM((1, ROWS), i32),
            pltpu.VMEM((N_DEV, ROWS), bf16),
            pltpu.VMEM((2, OWN * LANES, PAIR * MSG_R), bf16),
            pltpu.VMEM((OWN * LANES, OWN * LANES), bf16),
            pltpu.VMEM((128, 256), bf16),
            pltpu.VMEM((N_DEV, LANES), f32),
            pltpu.VMEM((CHUNKS, OWN, LANES), f32),
            pltpu.VMEM((CHUNKS, OWN, LANES), f32),
            pltpu.VMEM((NC, CHUNKS, LANES), f32),
            pltpu.VMEM((GROUP, CHUNKS, LANES), f32),
            pltpu.SemaphoreType.DMA,
            pltpu.SemaphoreType.DMA,
            pltpu.SemaphoreType.DMA((D_STEPS,)),
            pltpu.SemaphoreType.REGULAR,
            pltpu.SemaphoreType.DMA((2,)),
            pltpu.SemaphoreType.DMA((2,)),
            pltpu.SemaphoreType.DMA,
            pltpu.SemaphoreType.DMA((E_STEPS,)),
            pltpu.SemaphoreType.DMA((2,)),
            pltpu.SemaphoreType.DMA((2,)),
        ],
        compiler_params=pltpu.CompilerParams(
            collective_id=1, has_side_effects=True, vmem_limit_bytes=48 * 1024 * 1024
        ),
    )(ids, embeds)


def padded_nearest(ids, embeds):
    return pl.pallas_call(
        padded_kernel,
        out_shape=jax.ShapeDtypeStruct((1, ROWS), jnp.float32),
        in_specs=[
            pl.BlockSpec(memory_space=pltpu.VMEM),
            pl.BlockSpec(memory_space=pl.ANY),
        ],
        out_specs=pl.BlockSpec(memory_space=pltpu.VMEM),
        scratch_shapes=[
            pltpu.VMEM((ROWS, FEAT), jnp.bfloat16),
            pltpu.VMEM((N_DEV, MSG_R, MSG_C), jnp.bfloat16),
            pltpu.VMEM((N_DEV, MSG_R, MSG_C), jnp.bfloat16),
            pltpu.VMEM((OWN, CHUNKS * STRIDE, FEAT), jnp.bfloat16),
            pltpu.VMEM((OWN, 1, CHUNKS * STRIDE), jnp.float32),
            pltpu.VMEM((OWN, 1, CHUNKS * STRIDE), jnp.float32),
            pltpu.VMEM((1, ROWS), jnp.int32),
            pltpu.VMEM((N_DEV, ROWS), jnp.bfloat16),
            pltpu.VMEM((4, GROUP * MSG_R, OWN * SLOTS), jnp.bfloat16),
            pltpu.VMEM((4, OWN * STRIDE, GROUP * MSG_R), jnp.bfloat16),
            pltpu.VMEM((128, 256), jnp.bfloat16),
            pltpu.VMEM((N_DEV, 128), jnp.float32),
            pltpu.VMEM((CHUNKS, OWN, 128), jnp.float32),
            pltpu.VMEM((CHUNKS, OWN, 128), jnp.float32),
            pltpu.VMEM((NC, CHUNKS, 128), jnp.float32),
            pltpu.VMEM((GROUP, CHUNKS, 128), jnp.float32),
            pltpu.SemaphoreType.DMA,
            pltpu.SemaphoreType.DMA,
            pltpu.SemaphoreType.DMA((CHUNKS,)),
            pltpu.SemaphoreType.REGULAR,
            pltpu.SemaphoreType.DMA((2,)),
            pltpu.SemaphoreType.DMA((2,)),
        ],
        compiler_params=pltpu.CompilerParams(
            collective_id=0, has_side_effects=True, vmem_limit_bytes=48 * 1024 * 1024
        ),
    )(ids, embeds)


def on_device(embeds, cluster):
    ids = cluster.reshape(1, ROWS)
    nearest, over = fast_nearest(ids, embeds)
    nearest = lax.cond(
        over[0, 0] > 0.5, lambda: padded_nearest(ids, embeds), lambda: nearest
    )
    return nearest.reshape(ROWS)


def solution(mesh):
    return jax.shard_map(
        on_device,
        mesh=mesh,
        in_specs=(P(("grp", "dev"), None), P(("grp", "dev"), None)),
        out_specs=P(("grp", "dev")),
        check_vma=False,
    )
```

```python
import functools

import jax
import jax.numpy as jnp
from jax import lax
from jax.experimental import pallas as pl
from jax.experimental.pallas import tpu as pltpu
from jax.sharding import PartitionSpec as P

LOGICAL = pl.DeviceIdType.LOGICAL
NY, NX, NZ, NC = 4, 4, 8, 2
N_DEV = NY * NX * NZ * NC
ROWS, FEAT = 2048, 512
OWN, CAP = 2, 6
N_CL = OWN * N_DEV
GROUP = NZ * NC
CHUNKS = N_DEV // GROUP
SLOTS = GROUP * CAP
STRIDE = 128
HALF = NZ * CAP
MSG_R, MSG_C = 16, 384
HEAD = 384
DEAD = 4.0
FAR = -1e6
DIRECT = 4
EXTRA = CAP - DIRECT
SPILL = 64
PAIR = 2 * GROUP
OWNERS = NY * NX * NC
D_STEPS = N_DEV // PAIR
E_STEPS = 4
EARLY = 1
MEANWHILE = 12
Z_ORDER = (1, 7, 2, 6, 3, 5, 4)
AHEAD = 6
BEFORE = 5
E_OWN = OWNERS // E_STEPS
LANES = 128
WIDTH = (D_STEPS + E_STEPS) * LANES


def iota(shape, dim):
    return lax.broadcasted_iota(jnp.int32, shape, dim)


def ones_at(mask):
    return jnp.where(mask, 1.0, 0.0).astype(jnp.bfloat16)


def dot(a, b):
    return jnp.dot(a, b, preferred_element_type=jnp.float32)


def dot_t(a, b):
    return lax.dot_general(a, b, (((1,), (1,)), ((), ())), preferred_element_type=jnp.float32)


def split3(v):
    hi = v.astype(jnp.bfloat16)
    rest = v - hi.astype(jnp.float32)
    mid = rest.astype(jnp.bfloat16)
    lo = (rest - mid.astype(jnp.float32)).astype(jnp.bfloat16)
    return hi, mid, lo


def padded_kernel(
    ids_ref, embeds_hbm, out_ref,
    embeds, send, recv, unit, bias, best, rank, pick,
    pack, unpack, tri, wanted, back_out, back_mid, back_half, back_in,
    load_sem, sent_sem, got_sem, in_sem, back_sent_sem, back_got_sem,
):
    my_y = lax.axis_index("grp")
    my_dev = lax.axis_index("dev")
    my_x = my_dev // (NZ * NC)
    my_z = (my_dev // NC) % NZ
    my_c = my_dev % NC

    load = pltpu.make_async_copy(embeds_hbm, embeds, load_sem)
    load.start()

    def plane(sign):
        return [
            (my_z + sign * (j % NZ) + NZ) % NZ * NC + (my_c + j // NZ) % NC for j in range(GROUP)
        ]

    def column(g, sign):
        y = (my_y + sign * (g // NX) + NY) % NY
        x = (my_x + sign * (g % NX) + NX) % NX
        return (y * NX + x) * (NZ * NC)

    near = plane(1)
    here = column(0, 1)

    barrier = pltpu.get_barrier_semaphore()
    for j in range(1, GROUP):
        pl.semaphore_signal(barrier, inc=1, device_id=here + near[j], device_id_type=LOGICAL)
    for g in range(1, CHUNKS):
        pl.semaphore_signal(
            barrier, inc=1, device_id=column(g, 1) + near[0], device_id_type=LOGICAL
        )

    tri[...] = ones_at(
        (iota((128, 256), 0) < iota((128, 256), 1)) | (iota((128, 256), 1) >= 128)
    )

    ids = ids_ref[...]
    owner = ids >> 1
    sub = ids & 1
    dy = ((owner >> 6) - my_y) & (NY - 1)
    dx = ((owner >> 4) - my_x) & (NX - 1)
    dz = ((owner >> 1) - my_z) & (NZ - 1)
    dc = (owner - my_c) & (NC - 1)
    chunk = dy * NX + dx
    member_of = dc * NZ + dz
    rank[...] = jnp.zeros((1, ROWS), jnp.int32)

    def block_matrix(rows, slots_dim, which):
        block = iota(rows, 1 - slots_dim)
        s = iota(rows, slots_dim)
        peer = block // MSG_R
        i = block % MSG_R
        if which == 0:
            q, ok = i, i < OWN * CAP
        else:
            q, ok = 3 * (i - OWN * CAP) + (which - 1), i >= OWN * CAP
        return peer, q, ok, s

    for which in range(4):
        peer, q, ok, s = block_matrix((GROUP * MSG_R, OWN * SLOTS), 1, which)
        pack[which] = ones_at(ok & (s == (q // CAP) * SLOTS + peer * CAP + q % CAP))

    def make_chunk(g):
        mine = chunk == g
        member = iota((OWN * GROUP, ROWS), 0) == jnp.where(mine, sub * GROUP + member_of, -1)
        blocks = [slice(b * 128, (b + 1) * 128) for b in range(ROWS // 128)]
        flags = ones_at(member)
        sums = dot(jnp.concatenate([flags[:, b] for b in blocks], axis=0), tri[...])
        seen = jnp.zeros((OWN * GROUP, 128), jnp.float32)
        ranks = []
        for n, b in enumerate(blocks):
            part = sums[n * OWN * GROUP : (n + 1) * OWN * GROUP]
            ranks.append(
                jnp.sum(
                    jnp.where(member[:, b], part[:, :128] + seen, 0.0), axis=0, keepdims=True
                )
            )
            seen = seen + part[:, 128:]
        ranks = jnp.concatenate(ranks, axis=1).astype(jnp.int32)
        rank[...] += ranks
        place = jnp.where(mine, sub * SLOTS + member_of * CAP + ranks, -1)

        hit = iota((OWN * SLOTS, ROWS), 0) == place
        chosen = jnp.where(hit, 1.0, 0.0)
        live = jnp.sum(chosen, axis=1, keepdims=True)
        rows = dot(chosen.astype(jnp.bfloat16), embeds[...])
        rows = rows * lax.rsqrt(jnp.sum(rows * rows, axis=1, keepdims=True) + 1e-06)
        first = (iota((OWN * SLOTS, FEAT), 1) == 0) & (live < 0.5)
        rows = jnp.where(first, DEAD, rows).astype(jnp.bfloat16)
        tail = rows[:, HEAD:]
        for c in range(3):
            lanes = slice(c * 128, (c + 1) * 128)
            block = dot(pack[0], rows[:, lanes]) + dot(pack[1 + c], tail)
            send[pl.ds(g * GROUP, GROUP), :, lanes] = block.astype(jnp.bfloat16).reshape(
                GROUP, MSG_R, 128
            )

    def send_chunk(g, first):
        base = column(g, 1)
        for j in range(first, GROUP):
            k = g * GROUP + j
            pltpu.make_async_remote_copy(
                src_ref=send.at[k], dst_ref=recv.at[k], send_sem=sent_sem, recv_sem=got_sem.at[g],
                device_id=base + near[j], device_id_type=LOGICAL,
            ).start()

    pl.semaphore_wait(barrier, GROUP - 1 + CHUNKS - 1)
    for g in range(1, CHUNKS):
        pl.semaphore_signal(in_sem, inc=1, device_id=column(g, 1) + near[0], device_id_type=LOGICAL)
    load.wait()
    make_chunk(0)
    send_chunk(0, 1)
    pltpu.make_async_copy(send.at[0], recv.at[0], got_sem.at[0]).start()

    pl.semaphore_wait(in_sem, CHUNKS - 1)

    def send_step(g, carry):
        make_chunk(g)
        send_chunk(g, 0)
        return carry

    lax.fori_loop(1, CHUNKS, send_step, 0)

    for s in range(OWN):
        unit[s] = jnp.zeros((CHUNKS * STRIDE, FEAT), jnp.bfloat16)
        bias[s] = jnp.full((1, CHUNKS * STRIDE), FAR, jnp.float32)
        best[s] = jnp.full((1, CHUNKS * STRIDE), -1.0, jnp.float32)
    for which in range(4):
        peer, q, ok, s = block_matrix((OWN * STRIDE, GROUP * MSG_R), 0, which)
        unpack[which] = ones_at(ok & (s == (q // CAP) * STRIDE + peer * CAP + q % CAP))
    pick[...] = ones_at(iota((N_DEV, ROWS), 0) == member_of * CHUNKS + chunk)
    lane = iota((N_DEV, 128), 1)
    wanted[...] = jnp.where(
        ((lane % HALF) // CAP == (iota((N_DEV, 128), 0) // CHUNKS) % NZ) & (lane < OWN * HALF),
        1.0,
        0.0,
    )

    def got_step(g, carry):
        mine = pl.ds(g * GROUP, GROUP)
        pltpu.make_async_copy(recv.at[mine], recv.at[mine], got_sem.at[g]).wait()
        block = recv[mine].reshape(GROUP * MSG_R, MSG_C)
        head = dot(unpack[0], block)
        tail = (
            dot(unpack[1], block[:, :128])
            + dot(unpack[2], block[:, 128:256])
            + dot(unpack[3], block[:, 256:])
        )
        at = pl.ds(pl.multiple_of(g * STRIDE, STRIDE), STRIDE)
        for s in range(OWN):
            part = slice(s * STRIDE, (s + 1) * STRIDE)
            new = jnp.concatenate([head[part], tail[part]], axis=1).astype(jnp.bfloat16)
            empty = (head[part, :1] > 2.0) | (iota((STRIDE, 1), 0) >= SLOTS)
            new_bias = jnp.where(empty, FAR, 0.0)
            same = iota((STRIDE, STRIDE), 0) == iota((STRIDE, STRIDE), 1)
            new_row = jnp.sum(jnp.where(same, new_bias, 0.0), axis=0, keepdims=True)
            sims = dot_t(new, unit[s])
            by_new = jnp.max(sims + new_bias, axis=0, keepdims=True)
            by_old = jnp.full((STRIDE, STRIDE), -1.0, jnp.float32)
            for h in range(CHUNKS):
                lanes = slice(h * STRIDE, (h + 1) * STRIDE)
                by_old = jnp.maximum(by_old, sims[:, lanes] + bias[s, :, lanes])
            by_old = jnp.max(by_old.T, axis=0, keepdims=True)
            among = jnp.where(same, -1.0, dot_t(new, new) + new_bias)
            arrived = iota((1, CHUNKS * STRIDE), 1) < g * STRIDE
            best[s] = jnp.maximum(best[s], jnp.where(arrived, by_new, -1.0))
            best[s, :, at] = jnp.maximum(
                jnp.maximum(by_old, jnp.max(among, axis=0, keepdims=True)), -1.0
            )
            unit[s, at] = new
            bias[s, :, at] = new_row
        return carry

    lax.fori_loop(0, CHUNKS, got_step, 0)

    far = plane(-1)
    for s in range(OWN):
        for g in range(CHUNKS):
            back_out[g, s : s + 1] = best[s, :, g * STRIDE : (g + 1) * STRIDE]
    for g in range(1, CHUNKS):
        pltpu.make_async_remote_copy(
            src_ref=back_out.at[g], dst_ref=back_mid.at[g],
            send_sem=back_sent_sem.at[0], recv_sem=back_got_sem.at[0],
            device_id=column(g, -1) + far[0], device_id_type=LOGICAL,
        ).start()
    back_mid[0] = back_out[0]
    rest = pl.ds(1, CHUNKS - 1)
    pltpu.make_async_copy(back_mid.at[rest], back_mid.at[rest], back_got_sem.at[0]).wait()
    lane = iota((CHUNKS, 128), 1)
    first, second = back_mid[:, 0, :], back_mid[:, 1, :]
    back_half[0] = jnp.where(lane < HALF, first, pltpu.roll(second, HALF, 1))
    back_half[1] = jnp.where(lane < HALF, pltpu.roll(first, 128 - HALF, 1), second)
    for j in range(1, GROUP):
        pltpu.make_async_remote_copy(
            src_ref=back_half.at[j // NZ], dst_ref=back_in.at[j],
            send_sem=back_sent_sem.at[1], recv_sem=back_got_sem.at[1],
            device_id=here + far[j], device_id_type=LOGICAL,
        ).start()
    back_in[0] = back_half[0]
    rest = pl.ds(1, GROUP - 1)
    pltpu.make_async_copy(back_in.at[rest], back_in.at[rest], back_got_sem.at[1]).wait()

    at_row, at_lane = iota((16, 128), 0), iota((16, 128), 1)
    by_rank = ones_at(
        (at_lane < OWN * HALF) & (at_row == at_lane // HALF * 8 + at_lane % HALF % CAP)
    )
    values = jnp.where(wanted[...] > 0.5, back_in[...].reshape(N_DEV, 128), 0.0)
    hi, mid, lo = split3(values)
    answers = dot_t(by_rank, hi) + dot_t(by_rank, mid) + dot_t(by_rank, lo)
    hi, mid, lo = split3(answers)
    spread = dot(hi, pick[...]) + dot(mid, pick[...]) + dot(lo, pick[...])
    row = (ids_ref[...] & 1) * 8 + rank[...]
    out_ref[...] = jnp.sum(
        jnp.where(iota((16, ROWS), 0) == row, spread, 0.0), axis=0, keepdims=True
    )

    others = pl.ds(0, N_DEV - 1)
    pltpu.make_async_copy(send.at[others], send.at[others], sent_sem).wait()
    pltpu.make_async_copy(back_out.at[rest], back_out.at[rest], back_sent_sem.at[0]).wait()
    pltpu.make_async_copy(back_in.at[rest], back_in.at[rest], back_sent_sem.at[1]).wait()


def fast_kernel(
    ids_ref, embeds_hbm, out_ref, over_ref,
    embeds, send, recv, spill_out, spill_in, tag_out, tag_in, extra_out, extra_in,
    unit, bias, best, best_rows, rank, pick, undirect, unextra, tri, wanted,
    back_out, back_mid, back_half, back_in,
    load_sem, sent_sem, got_sem, in_sem, spill_sem, tag_sem, extra_sent_sem, extra_sem,
    back_sent_sem, back_got_sem,
):
    my_y = lax.axis_index("grp")
    my_dev = lax.axis_index("dev")
    my_x = my_dev // (NZ * NC)
    my_z = (my_dev // NC) % NZ
    my_c = my_dev % NC

    load = pltpu.make_async_copy(embeds_hbm, embeds, load_sem)
    load.start()

    def plane(sign):
        return [
            (my_z + sign * (j % NZ) + NZ) % NZ * NC + (my_c + j // NZ) % NC for j in range(GROUP)
        ]

    def column(g, sign):
        y = (my_y + sign * (g // NX) + NY) % NY
        x = (my_x + sign * (g % NX) + NX) % NX
        return (y * NX + x) * (NZ * NC)

    near = plane(1)
    here = column(0, 1)

    barrier = pltpu.get_barrier_semaphore()
    for j in range(1, GROUP):
        pl.semaphore_signal(barrier, inc=1, device_id=here + near[j], device_id_type=LOGICAL)
    for g in range(1, CHUNKS):
        pl.semaphore_signal(
            barrier, inc=1, device_id=column(g, 1) + near[0], device_id_type=LOGICAL
        )

    tri[...] = ones_at(
        (iota((128, 256), 0) < iota((128, 256), 1)) | (iota((128, 256), 1) >= 128)
    )

    ids = ids_ref[...]
    owner = ids >> 1
    sub = ids & 1
    dy = ((owner >> 6) - my_y) & (NY - 1)
    dx = ((owner >> 4) - my_x) & (NX - 1)
    dz = ((owner >> 1) - my_z) & (NZ - 1)
    dc = (owner - my_c) & (NC - 1)
    chunk = dy * NX + dx
    member_of = dc * NZ + dz
    rank[...] = jnp.zeros((1, ROWS), jnp.int32)

    def count_before(key, kinds):
        member = iota((kinds, ROWS), 0) == key
        blocks = [slice(b * 128, (b + 1) * 128) for b in range(ROWS // 128)]
        flags = ones_at(member)
        sums = dot(jnp.concatenate([flags[:, b] for b in blocks], axis=0), tri[...])
        seen = jnp.zeros((kinds, 128), jnp.float32)
        before = []
        for n, b in enumerate(blocks):
            part = sums[n * kinds : (n + 1) * kinds]
            before.append(
                jnp.sum(
                    jnp.where(member[:, b], part[:, :128] + seen, 0.0), axis=0, keepdims=True
                )
            )
            seen = seen + part[:, 128:]
        return jnp.concatenate(before, axis=1).astype(jnp.int32), seen

    def rank_chunk(g):
        key = jnp.where(chunk == g, sub * GROUP + member_of, -1)
        rank[...] += count_before(key, OWN * GROUP)[0]

    def chosen_rows(place, amount):
        chosen = jnp.where(iota((amount, ROWS), 0) == place, 1.0, 0.0)
        rows = dot(chosen.astype(jnp.bfloat16), embeds[...])
        rows = rows * lax.rsqrt(jnp.sum(rows * rows, axis=1, keepdims=True) + 1e-06)
        return chosen, rows

    def mark_empty(rows, chosen):
        empty = jnp.sum(chosen, axis=1, keepdims=True) < 0.5
        return jnp.where((iota(rows.shape, 1) == 0) & empty, DEAD, rows)

    def make_direct(first, chunks):
        order = chunk - first
        mine = (order >= 0) & (order < chunks) & (rank[...] < DIRECT)
        slot = ((order * GROUP + member_of) * OWN + sub) * DIRECT + rank[...]
        chosen, rows = chosen_rows(jnp.where(mine, slot, -1), chunks * GROUP * OWN * DIRECT)
        rows = mark_empty(rows, chosen).reshape(chunks * GROUP, OWN * DIRECT, FEAT)
        block = jnp.concatenate([rows[:, :, : FEAT // 2], rows[:, :, FEAT // 2 :]], axis=1)
        send[pl.ds(first * GROUP, chunks * GROUP)] = block.astype(jnp.bfloat16)

    def send_chunk(g, first, sem):
        base = column(g, 1)
        for j in range(first, GROUP):
            k = g * GROUP + j
            pltpu.make_async_remote_copy(
                src_ref=send.at[k], dst_ref=recv.at[k], send_sem=sent_sem, recv_sem=got_sem.at[sem],
                device_id=base + near[j], device_id_type=LOGICAL,
            ).start()

    def rank_step(g, carry):
        rank_chunk(g)
        return carry

    def send_step(q, carry):
        make_direct(2 * q, 2)
        send_chunk(2 * q, 0, q)
        send_chunk(2 * q + 1, 0, q)
        return carry

    rank_chunk(0)
    rank_chunk(1)
    load.wait()
    make_direct(0, 2)
    pl.semaphore_wait(barrier, GROUP - 1 + CHUNKS - 1)
    for g in range(1, CHUNKS):
        pl.semaphore_signal(in_sem, inc=1, device_id=column(g, 1) + near[0], device_id_type=LOGICAL)
    send_chunk(0, 1, 0)
    pltpu.make_async_copy(send.at[0], recv.at[0], got_sem.at[0]).start()
    lax.fori_loop(2, MEANWHILE, rank_step, 0)
    pl.semaphore_wait(in_sem, CHUNKS - 1)
    send_chunk(1, 0, 0)
    lax.fori_loop(MEANWHILE, CHUNKS, rank_step, 0)

    beyond = rank[...] >= DIRECT
    spot, totals = count_before(jnp.where(beyond, dz, -1), 2 * NZ)
    over = jnp.max(totals, axis=(0, 1), keepdims=True) > SPILL
    over = jnp.where(over, 1.0, 0.0)
    place = jnp.where(beyond & (spot < SPILL), dz * SPILL + spot, -1)
    chosen, rows = chosen_rows(place, NZ * SPILL)
    spill_out[...] = rows.astype(jnp.bfloat16).reshape(NZ, SPILL, FEAT)
    spill_in[0] = rows[:SPILL].astype(jnp.bfloat16)
    label = ((chunk * NC + dc) * OWN + sub) * EXTRA + rank[...] - DIRECT + 1
    labels = jnp.sum(jnp.where(chosen > 0.5, label.astype(jnp.float32), 0.0), axis=1, keepdims=True)
    same = iota((LANES, LANES), 0) == iota((LANES, LANES), 1)
    for b in range(NZ * SPILL // LANES):
        part = labels[b * LANES : (b + 1) * LANES]
        line = jnp.sum(jnp.where(same, part, 0.0), axis=0, keepdims=True)
        tag_out[2 * b] = line.astype(jnp.int32)
        tag_out[2 * b + 1] = pltpu.roll(line, SPILL, 1).astype(jnp.int32)
    tag_in[0] = tag_out[0]
    for piece in range(SPILL // MSG_R):
        for d in Z_ORDER:
            rows = pl.ds(piece * MSG_R, MSG_R)
            pltpu.make_async_remote_copy(
                src_ref=spill_out.at[d, rows], dst_ref=spill_in.at[d, rows],
                send_sem=spill_sem.at[0], recv_sem=spill_sem.at[1],
                device_id=here + near[d], device_id_type=LOGICAL,
            ).start()
            if piece == 0:
                pltpu.make_async_remote_copy(
                    src_ref=tag_out.at[d], dst_ref=tag_in.at[d],
                    send_sem=tag_sem.at[0], recv_sem=tag_sem.at[1],
                    device_id=here + near[d], device_id_type=LOGICAL,
                ).start()

    lax.fori_loop(EARLY, AHEAD, send_step, 0)

    others = pl.ds(1, NZ - 1)
    pltpu.make_async_copy(spill_in.at[others], spill_in.at[others], spill_sem.at[1]).wait()
    pltpu.make_async_copy(tag_in.at[others], tag_in.at[others], tag_sem.at[1]).wait()
    lane = iota((1, LANES), 1)
    onward = []
    for b in range(NZ // 2):
        line = jnp.where(lane < SPILL, tag_in[2 * b], pltpu.roll(tag_in[2 * b + 1], SPILL, 1))
        at = line - 1
        at = (at >> 2) * (NZ * OWN * EXTRA) + (2 * b + (lane >> 6)) * (OWN * EXTRA) + (at & 3)
        onward.append(jnp.where(line > 0, at, -1))
    onward = jnp.concatenate(onward, axis=1)

    def onward_step(e, carry):
        amount = E_OWN * NZ * OWN * EXTRA
        chosen = jnp.where(iota((amount, NZ * SPILL), 0) + e * amount == onward, 1.0, 0.0)
        rows = dot(chosen.astype(jnp.bfloat16), spill_in[...].reshape(NZ * SPILL, FEAT))
        rows = mark_empty(rows, chosen).astype(jnp.bfloat16)
        extra_out[pl.ds(e * E_OWN, E_OWN)] = rows.reshape(E_OWN, NZ * OWN * EXTRA, FEAT)
        return carry

    lax.fori_loop(0, E_STEPS, onward_step, 0)
    pltpu.make_async_copy(extra_out.at[0], extra_in.at[0], extra_sem.at[0]).start()
    for j in range(E_OWN):
        for e in (1, 3, 2, 0):
            k = e * E_OWN + j
            if k > 0:
                pltpu.make_async_remote_copy(
                    src_ref=extra_out.at[k], dst_ref=extra_in.at[k],
                    send_sem=extra_sent_sem, recv_sem=extra_sem.at[e],
                    device_id=column(k // NC, 1) + near[j % NC * NZ], device_id_type=LOGICAL,
                ).start()

    lax.fori_loop(AHEAD, D_STEPS, send_step, 0)

    for s in range(OWN):
        unit[s] = jnp.zeros((WIDTH, FEAT), jnp.bfloat16)
        bias[s] = jnp.full((1, WIDTH), FAR, jnp.float32)
        best[s] = jnp.full((1, WIDTH), -1.0, jnp.float32)
    to, frm = iota((OWN * LANES, PAIR * MSG_R), 0), iota((OWN * LANES, PAIR * MSG_R), 1)
    slot = to % LANES
    at = slot // DIRECT * MSG_R + to // LANES * DIRECT + slot % DIRECT
    undirect[0] = ones_at(frm == at)
    undirect[1] = ones_at(frm == at + OWN * DIRECT)
    to, frm = iota((OWN * LANES, OWN * LANES), 0), iota((OWN * LANES, OWN * LANES), 1)
    slot = to % LANES
    unextra[...] = ones_at(
        frm == slot // EXTRA * (OWN * EXTRA) + to // LANES * EXTRA + slot % EXTRA
    )
    pick[...] = ones_at(iota((N_DEV, ROWS), 0) == member_of * CHUNKS + chunk)
    lane = iota((N_DEV, LANES), 1)
    lane_dz = jnp.where(lane < 64, lane % 32 // DIRECT, lane % 16 // EXTRA)
    wanted[...] = jnp.where(
        (lane_dz == (iota((N_DEV, LANES), 0) // CHUNKS) % NZ) & (lane < 96), 1.0, 0.0
    )

    def compare(t, both):
        at = pl.ds(pl.multiple_of(t * LANES, LANES), LANES)
        for s in range(OWN):
            part = both[s * LANES : (s + 1) * LANES]
            new = part.astype(jnp.bfloat16)
            new_bias = jnp.where(part[:, :1] > 2.0, FAR, 0.0)
            same = iota((LANES, LANES), 0) == iota((LANES, LANES), 1)
            new_row = jnp.sum(jnp.where(same, new_bias, 0.0), axis=0, keepdims=True)
            sims = dot_t(new, unit[s])
            by_new = jnp.max(sims + new_bias, axis=0, keepdims=True)
            by_old = jnp.full((LANES, LANES), -1.0, jnp.float32)
            for h in range(D_STEPS + E_STEPS):
                lanes = slice(h * LANES, (h + 1) * LANES)
                by_old = jnp.maximum(by_old, sims[:, lanes] + bias[s, :, lanes])
            by_old = jnp.max(by_old.T, axis=0, keepdims=True)
            among = jnp.where(same, -1.0, dot_t(new, new) + new_bias)
            best[s] = jnp.maximum(best[s], jnp.where(bias[s] > -1.0, by_new, -1.0))
            best[s, :, at] = jnp.maximum(
                jnp.maximum(by_old, jnp.max(among, axis=0, keepdims=True)), -1.0
            )
            unit[s, at] = new
            bias[s, :, at] = new_row

    def direct_step(q, carry):
        mine = pl.ds(q * PAIR, PAIR)
        pltpu.make_async_copy(recv.at[mine], recv.at[mine], got_sem.at[q]).wait()
        block = recv[mine].reshape(PAIR * MSG_R, FEAT // 2)
        compare(q, jnp.concatenate([dot(undirect[0], block), dot(undirect[1], block)], axis=1))
        return carry

    def extra_step(e, carry):
        mine = pl.ds(e * E_OWN, E_OWN)
        pltpu.make_async_copy(extra_in.at[mine], extra_in.at[mine], extra_sem.at[e]).wait()
        block = extra_in[mine].reshape(OWN * LANES, FEAT)
        compare(D_STEPS + e, dot(unextra[...], block))
        return carry

    lax.fori_loop(0, BEFORE, direct_step, 0)
    lax.fori_loop(0, E_STEPS, extra_step, 0)
    lax.fori_loop(BEFORE, D_STEPS, direct_step, 0)

    far = plane(-1)
    for s in range(OWN):
        for t in range(D_STEPS + E_STEPS):
            best_rows[s, t : t + 1] = best[s, :, t * LANES : (t + 1) * LANES]
    lane = iota((D_STEPS, LANES), 1)
    first, second = best_rows[0, :D_STEPS], best_rows[1, :D_STEPS]
    even = jnp.where(lane < 64, first, pltpu.roll(second, 64, 1))
    odd = jnp.where(lane < 64, pltpu.roll(first, 64, 1), second)
    for q in range(D_STEPS):
        back_out[2 * q, 0:1] = even[q : q + 1]
        back_out[2 * q + 1, 0:1] = odd[q : q + 1]
    first, second = best_rows[0, D_STEPS:], best_rows[1, D_STEPS:]
    for r in range(4):
        line = jnp.where(
            lane < 32,
            first if r == 0 else pltpu.roll(first, 128 - 32 * r, 1),
            second if r == 1 else pltpu.roll(second, (160 - 32 * r) % 128, 1),
        )
        line = jnp.where(lane < 96, line, over)
        for e in range(E_STEPS):
            back_out[4 * e + r, 1:2] = line[e : e + 1]
    for g in range(1, CHUNKS):
        pltpu.make_async_remote_copy(
            src_ref=back_out.at[g], dst_ref=back_mid.at[g],
            send_sem=back_sent_sem.at[0], recv_sem=back_got_sem.at[0],
            device_id=column(g, -1) + far[0], device_id_type=LOGICAL,
        ).start()
    back_mid[0] = back_out[0]
    rest = pl.ds(1, CHUNKS - 1)
    pltpu.make_async_copy(back_mid.at[rest], back_mid.at[rest], back_got_sem.at[0]).wait()
    lane = iota((CHUNKS, LANES), 1)
    main, more = back_mid[:, 0, :], back_mid[:, 1, :]
    over = jnp.max(jnp.where(lane < 96, 0.0, more), axis=(0, 1), keepdims=True)
    for h in range(NC):
        line = jnp.where(lane < 96, pltpu.roll(more, 48 - 16 * h, 1), over)
        line = jnp.where(lane < 80, pltpu.roll(more, 64 - 16 * h, 1), line)
        line = jnp.where(lane < 64, pltpu.roll(main, 96 - 32 * h, 1), line)
        back_half[h] = jnp.where(lane < 32, main if h == 0 else pltpu.roll(main, 96, 1), line)
    for j in range(1, GROUP):
        pltpu.make_async_remote_copy(
            src_ref=back_half.at[j // NZ], dst_ref=back_in.at[j],
            send_sem=back_sent_sem.at[1], recv_sem=back_got_sem.at[1],
            device_id=here + far[j], device_id_type=LOGICAL,
        ).start()
    back_in[0] = back_half[0]
    rest = pl.ds(1, GROUP - 1)
    pltpu.make_async_copy(back_in.at[rest], back_in.at[rest], back_got_sem.at[1]).wait()

    at_row, lane = iota((16, LANES), 0), iota((16, LANES), 1)
    kind = jnp.where(
        lane < 64, lane // 32 * 8 + lane % DIRECT, (lane - 64) // 16 * 8 + DIRECT + lane % EXTRA
    )
    by_rank = ones_at((lane < 96) & (at_row == kind))
    everything = back_in[...].reshape(N_DEV, LANES)
    values = jnp.where(wanted[...] > 0.5, everything, 0.0)
    hi, mid, lo = split3(values)
    answers = dot_t(by_rank, hi) + dot_t(by_rank, mid) + dot_t(by_rank, lo)
    hi, mid, lo = split3(answers)
    spread = dot(hi, pick[...]) + dot(mid, pick[...]) + dot(lo, pick[...])
    row = (ids_ref[...] & 1) * 8 + rank[...]
    out_ref[...] = jnp.sum(
        jnp.where(iota((16, ROWS), 0) == row, spread, 0.0), axis=0, keepdims=True
    )
    lane = iota((N_DEV, LANES), 1)
    over = jnp.max(jnp.where(lane < 96, 0.0, everything), axis=(0, 1), keepdims=True)
    over_ref[...] = jnp.broadcast_to(over, (1, LANES))

    peers = pl.ds(1, N_DEV - 1)
    pltpu.make_async_copy(send.at[peers], send.at[peers], sent_sem).wait()
    pltpu.make_async_copy(spill_out.at[others], spill_out.at[others], spill_sem.at[0]).wait()
    pltpu.make_async_copy(tag_out.at[others], tag_out.at[others], tag_sem.at[0]).wait()
    peers = pl.ds(1, OWNERS - 1)
    pltpu.make_async_copy(extra_out.at[peers], extra_out.at[peers], extra_sent_sem).wait()
    pltpu.make_async_copy(back_out.at[rest], back_out.at[rest], back_sent_sem.at[0]).wait()
    pltpu.make_async_copy(back_in.at[rest], back_in.at[rest], back_sent_sem.at[1]).wait()


def fast_nearest(ids, embeds):
    bf16, f32, i32 = jnp.bfloat16, jnp.float32, jnp.int32
    return pl.pallas_call(
        fast_kernel,
        out_shape=(
            jax.ShapeDtypeStruct((1, ROWS), f32),
            jax.ShapeDtypeStruct((1, LANES), f32),
        ),
        in_specs=[
            pl.BlockSpec(memory_space=pltpu.VMEM),
            pl.BlockSpec(memory_space=pl.ANY),
        ],
        out_specs=(
            pl.BlockSpec(memory_space=pltpu.VMEM),
            pl.BlockSpec(memory_space=pltpu.VMEM),
        ),
        scratch_shapes=[
            pltpu.VMEM((ROWS, FEAT), bf16),
            pltpu.VMEM((N_DEV, MSG_R, FEAT // 2), bf16),
            pltpu.VMEM((N_DEV, MSG_R, FEAT // 2), bf16),
            pltpu.VMEM((NZ, SPILL, FEAT), bf16),
            pltpu.VMEM((NZ, SPILL, FEAT), bf16),
            pltpu.VMEM((NZ, 1, LANES), i32),
            pltpu.VMEM((NZ, 1, LANES), i32),
            pltpu.VMEM((OWNERS, NZ * OWN * EXTRA, FEAT), bf16),
            pltpu.VMEM((OWNERS, NZ * OWN * EXTRA, FEAT), bf16),
            pltpu.VMEM((OWN, WIDTH, FEAT), bf16),
            pltpu.VMEM((OWN, 1, WIDTH), f32),
            pltpu.VMEM((OWN, 1, WIDTH), f32),
            pltpu.VMEM((OWN, 2 * D_STEPS, LANES), f32),
            pltpu.VMEM((1, ROWS), i32),
            pltpu.VMEM((N_DEV, ROWS), bf16),
            pltpu.VMEM((2, OWN * LANES, PAIR * MSG_R), bf16),
            pltpu.VMEM((OWN * LANES, OWN * LANES), bf16),
            pltpu.VMEM((128, 256), bf16),
            pltpu.VMEM((N_DEV, LANES), f32),
            pltpu.VMEM((CHUNKS, OWN, LANES), f32),
            pltpu.VMEM((CHUNKS, OWN, LANES), f32),
            pltpu.VMEM((NC, CHUNKS, LANES), f32),
            pltpu.VMEM((GROUP, CHUNKS, LANES), f32),
            pltpu.SemaphoreType.DMA,
            pltpu.SemaphoreType.DMA,
            pltpu.SemaphoreType.DMA((D_STEPS,)),
            pltpu.SemaphoreType.REGULAR,
            pltpu.SemaphoreType.DMA((2,)),
            pltpu.SemaphoreType.DMA((2,)),
            pltpu.SemaphoreType.DMA,
            pltpu.SemaphoreType.DMA((E_STEPS,)),
            pltpu.SemaphoreType.DMA((2,)),
            pltpu.SemaphoreType.DMA((2,)),
        ],
        compiler_params=pltpu.CompilerParams(
            collective_id=1, has_side_effects=True, vmem_limit_bytes=48 * 1024 * 1024
        ),
    )(ids, embeds)


def padded_nearest(ids, embeds):
    return pl.pallas_call(
        padded_kernel,
        out_shape=jax.ShapeDtypeStruct((1, ROWS), jnp.float32),
        in_specs=[
            pl.BlockSpec(memory_space=pltpu.VMEM),
            pl.BlockSpec(memory_space=pl.ANY),
        ],
        out_specs=pl.BlockSpec(memory_space=pltpu.VMEM),
        scratch_shapes=[
            pltpu.VMEM((ROWS, FEAT), jnp.bfloat16),
            pltpu.VMEM((N_DEV, MSG_R, MSG_C), jnp.bfloat16),
            pltpu.VMEM((N_DEV, MSG_R, MSG_C), jnp.bfloat16),
            pltpu.VMEM((OWN, CHUNKS * STRIDE, FEAT), jnp.bfloat16),
            pltpu.VMEM((OWN, 1, CHUNKS * STRIDE), jnp.float32),
            pltpu.VMEM((OWN, 1, CHUNKS * STRIDE), jnp.float32),
            pltpu.VMEM((1, ROWS), jnp.int32),
            pltpu.VMEM((N_DEV, ROWS), jnp.bfloat16),
            pltpu.VMEM((4, GROUP * MSG_R, OWN * SLOTS), jnp.bfloat16),
            pltpu.VMEM((4, OWN * STRIDE, GROUP * MSG_R), jnp.bfloat16),
            pltpu.VMEM((128, 256), jnp.bfloat16),
            pltpu.VMEM((N_DEV, 128), jnp.float32),
            pltpu.VMEM((CHUNKS, OWN, 128), jnp.float32),
            pltpu.VMEM((CHUNKS, OWN, 128), jnp.float32),
            pltpu.VMEM((NC, CHUNKS, 128), jnp.float32),
            pltpu.VMEM((GROUP, CHUNKS, 128), jnp.float32),
            pltpu.SemaphoreType.DMA,
            pltpu.SemaphoreType.DMA,
            pltpu.SemaphoreType.DMA((CHUNKS,)),
            pltpu.SemaphoreType.REGULAR,
            pltpu.SemaphoreType.DMA((2,)),
            pltpu.SemaphoreType.DMA((2,)),
        ],
        compiler_params=pltpu.CompilerParams(
            collective_id=0, has_side_effects=True, vmem_limit_bytes=48 * 1024 * 1024
        ),
    )(ids, embeds)


def on_device(embeds, cluster):
    ids = cluster.reshape(1, ROWS)
    nearest, over = fast_nearest(ids, embeds)
    nearest = lax.cond(
        over[0, 0] > 0.5, lambda: padded_nearest(ids, embeds), lambda: nearest
    )
    return nearest.reshape(ROWS)


def solution(mesh):
    return jax.shard_map(
        on_device,
        mesh=mesh,
        in_specs=(P(("grp", "dev"), None), P(("grp", "dev"), None)),
        out_specs=P(("grp", "dev")),
        check_vma=False,
    )
```

```python
import functools

import jax
import jax.numpy as jnp
from jax import lax
from jax.experimental import pallas as pl
from jax.experimental.pallas import tpu as pltpu
from jax.sharding import PartitionSpec as P

LOGICAL = pl.DeviceIdType.LOGICAL
NY, NX, NZ, NC = 4, 4, 8, 2
N_DEV = NY * NX * NZ * NC
ROWS, FEAT = 2048, 512
OWN, CAP = 2, 6
N_CL = OWN * N_DEV
GROUP = NZ * NC
CHUNKS = N_DEV // GROUP
SLOTS = GROUP * CAP
STRIDE = 128
HALF = NZ * CAP
MSG_R, MSG_C = 16, 384
HEAD = 384
DEAD = 4.0
FAR = -1e6
DIRECT = 4
EXTRA = CAP - DIRECT
SPILL = 64
PAIR = 2 * GROUP
OWNERS = NY * NX * NC
D_STEPS = N_DEV // PAIR
E_STEPS = 4
EARLY = 1
MEANWHILE = 12
Z_ORDER = (1, 7, 2, 6, 3, 5, 4)
AHEAD = 6
BEFORE = 6
E_OWN = OWNERS // E_STEPS
LANES = 128
WIDTH = (D_STEPS + E_STEPS) * LANES


def iota(shape, dim):
    return lax.broadcasted_iota(jnp.int32, shape, dim)


def ones_at(mask):
    return jnp.where(mask, 1.0, 0.0).astype(jnp.bfloat16)


def dot(a, b):
    return jnp.dot(a, b, preferred_element_type=jnp.float32)


def dot_t(a, b):
    return lax.dot_general(a, b, (((1,), (1,)), ((), ())), preferred_element_type=jnp.float32)


def split3(v):
    hi = v.astype(jnp.bfloat16)
    rest = v - hi.astype(jnp.float32)
    mid = rest.astype(jnp.bfloat16)
    lo = (rest - mid.astype(jnp.float32)).astype(jnp.bfloat16)
    return hi, mid, lo


def padded_kernel(
    ids_ref, embeds_hbm, out_ref,
    embeds, send, recv, unit, bias, best, rank, pick,
    pack, unpack, tri, wanted, back_out, back_mid, back_half, back_in,
    load_sem, sent_sem, got_sem, in_sem, back_sent_sem, back_got_sem,
):
    my_y = lax.axis_index("grp")
    my_dev = lax.axis_index("dev")
    my_x = my_dev // (NZ * NC)
    my_z = (my_dev // NC) % NZ
    my_c = my_dev % NC

    load = pltpu.make_async_copy(embeds_hbm, embeds, load_sem)
    load.start()

    def plane(sign):
        return [
            (my_z + sign * (j % NZ) + NZ) % NZ * NC + (my_c + j // NZ) % NC for j in range(GROUP)
        ]

    def column(g, sign):
        y = (my_y + sign * (g // NX) + NY) % NY
        x = (my_x + sign * (g % NX) + NX) % NX
        return (y * NX + x) * (NZ * NC)

    near = plane(1)
    here = column(0, 1)

    barrier = pltpu.get_barrier_semaphore()
    for j in range(1, GROUP):
        pl.semaphore_signal(barrier, inc=1, device_id=here + near[j], device_id_type=LOGICAL)
    for g in range(1, CHUNKS):
        pl.semaphore_signal(
            barrier, inc=1, device_id=column(g, 1) + near[0], device_id_type=LOGICAL
        )

    tri[...] = ones_at(
        (iota((128, 256), 0) < iota((128, 256), 1)) | (iota((128, 256), 1) >= 128)
    )

    ids = ids_ref[...]
    owner = ids >> 1
    sub = ids & 1
    dy = ((owner >> 6) - my_y) & (NY - 1)
    dx = ((owner >> 4) - my_x) & (NX - 1)
    dz = ((owner >> 1) - my_z) & (NZ - 1)
    dc = (owner - my_c) & (NC - 1)
    chunk = dy * NX + dx
    member_of = dc * NZ + dz
    rank[...] = jnp.zeros((1, ROWS), jnp.int32)

    def block_matrix(rows, slots_dim, which):
        block = iota(rows, 1 - slots_dim)
        s = iota(rows, slots_dim)
        peer = block // MSG_R
        i = block % MSG_R
        if which == 0:
            q, ok = i, i < OWN * CAP
        else:
            q, ok = 3 * (i - OWN * CAP) + (which - 1), i >= OWN * CAP
        return peer, q, ok, s

    for which in range(4):
        peer, q, ok, s = block_matrix((GROUP * MSG_R, OWN * SLOTS), 1, which)
        pack[which] = ones_at(ok & (s == (q // CAP) * SLOTS + peer * CAP + q % CAP))

    def make_chunk(g):
        mine = chunk == g
        member = iota((OWN * GROUP, ROWS), 0) == jnp.where(mine, sub * GROUP + member_of, -1)
        blocks = [slice(b * 128, (b + 1) * 128) for b in range(ROWS // 128)]
        flags = ones_at(member)
        sums = dot(jnp.concatenate([flags[:, b] for b in blocks], axis=0), tri[...])
        seen = jnp.zeros((OWN * GROUP, 128), jnp.float32)
        ranks = []
        for n, b in enumerate(blocks):
            part = sums[n * OWN * GROUP : (n + 1) * OWN * GROUP]
            ranks.append(
                jnp.sum(
                    jnp.where(member[:, b], part[:, :128] + seen, 0.0), axis=0, keepdims=True
                )
            )
            seen = seen + part[:, 128:]
        ranks = jnp.concatenate(ranks, axis=1).astype(jnp.int32)
        rank[...] += ranks
        place = jnp.where(mine, sub * SLOTS + member_of * CAP + ranks, -1)

        hit = iota((OWN * SLOTS, ROWS), 0) == place
        chosen = jnp.where(hit, 1.0, 0.0)
        live = jnp.sum(chosen, axis=1, keepdims=True)
        rows = dot(chosen.astype(jnp.bfloat16), embeds[...])
        rows = rows * lax.rsqrt(jnp.sum(rows * rows, axis=1, keepdims=True) + 1e-06)
        first = (iota((OWN * SLOTS, FEAT), 1) == 0) & (live < 0.5)
        rows = jnp.where(first, DEAD, rows).astype(jnp.bfloat16)
        tail = rows[:, HEAD:]
        for c in range(3):
            lanes = slice(c * 128, (c + 1) * 128)
            block = dot(pack[0], rows[:, lanes]) + dot(pack[1 + c], tail)
            send[pl.ds(g * GROUP, GROUP), :, lanes] = block.astype(jnp.bfloat16).reshape(
                GROUP, MSG_R, 128
            )

    def send_chunk(g, first):
        base = column(g, 1)
        for j in range(first, GROUP):
            k = g * GROUP + j
            pltpu.make_async_remote_copy(
                src_ref=send.at[k], dst_ref=recv.at[k], send_sem=sent_sem, recv_sem=got_sem.at[g],
                device_id=base + near[j], device_id_type=LOGICAL,
            ).start()

    pl.semaphore_wait(barrier, GROUP - 1 + CHUNKS - 1)
    for g in range(1, CHUNKS):
        pl.semaphore_signal(in_sem, inc=1, device_id=column(g, 1) + near[0], device_id_type=LOGICAL)
    load.wait()
    make_chunk(0)
    send_chunk(0, 1)
    pltpu.make_async_copy(send.at[0], recv.at[0], got_sem.at[0]).start()

    pl.semaphore_wait(in_sem, CHUNKS - 1)

    def send_step(g, carry):
        make_chunk(g)
        send_chunk(g, 0)
        return carry

    lax.fori_loop(1, CHUNKS, send_step, 0)

    for s in range(OWN):
        unit[s] = jnp.zeros((CHUNKS * STRIDE, FEAT), jnp.bfloat16)
        bias[s] = jnp.full((1, CHUNKS * STRIDE), FAR, jnp.float32)
        best[s] = jnp.full((1, CHUNKS * STRIDE), -1.0, jnp.float32)
    for which in range(4):
        peer, q, ok, s = block_matrix((OWN * STRIDE, GROUP * MSG_R), 0, which)
        unpack[which] = ones_at(ok & (s == (q // CAP) * STRIDE + peer * CAP + q % CAP))
    pick[...] = ones_at(iota((N_DEV, ROWS), 0) == member_of * CHUNKS + chunk)
    lane = iota((N_DEV, 128), 1)
    wanted[...] = jnp.where(
        ((lane % HALF) // CAP == (iota((N_DEV, 128), 0) // CHUNKS) % NZ) & (lane < OWN * HALF),
        1.0,
        0.0,
    )

    def got_step(g, carry):
        mine = pl.ds(g * GROUP, GROUP)
        pltpu.make_async_copy(recv.at[mine], recv.at[mine], got_sem.at[g]).wait()
        block = recv[mine].reshape(GROUP * MSG_R, MSG_C)
        head = dot(unpack[0], block)
        tail = (
            dot(unpack[1], block[:, :128])
            + dot(unpack[2], block[:, 128:256])
            + dot(unpack[3], block[:, 256:])
        )
        at = pl.ds(pl.multiple_of(g * STRIDE, STRIDE), STRIDE)
        for s in range(OWN):
            part = slice(s * STRIDE, (s + 1) * STRIDE)
            new = jnp.concatenate([head[part], tail[part]], axis=1).astype(jnp.bfloat16)
            empty = (head[part, :1] > 2.0) | (iota((STRIDE, 1), 0) >= SLOTS)
            new_bias = jnp.where(empty, FAR, 0.0)
            same = iota((STRIDE, STRIDE), 0) == iota((STRIDE, STRIDE), 1)
            new_row = jnp.sum(jnp.where(same, new_bias, 0.0), axis=0, keepdims=True)
            sims = dot_t(new, unit[s])
            by_new = jnp.max(sims + new_bias, axis=0, keepdims=True)
            by_old = jnp.full((STRIDE, STRIDE), -1.0, jnp.float32)
            for h in range(CHUNKS):
                lanes = slice(h * STRIDE, (h + 1) * STRIDE)
                by_old = jnp.maximum(by_old, sims[:, lanes] + bias[s, :, lanes])
            by_old = jnp.max(by_old.T, axis=0, keepdims=True)
            among = jnp.where(same, -1.0, dot_t(new, new) + new_bias)
            arrived = iota((1, CHUNKS * STRIDE), 1) < g * STRIDE
            best[s] = jnp.maximum(best[s], jnp.where(arrived, by_new, -1.0))
            best[s, :, at] = jnp.maximum(
                jnp.maximum(by_old, jnp.max(among, axis=0, keepdims=True)), -1.0
            )
            unit[s, at] = new
            bias[s, :, at] = new_row
        return carry

    lax.fori_loop(0, CHUNKS, got_step, 0)

    far = plane(-1)
    for s in range(OWN):
        for g in range(CHUNKS):
            back_out[g, s : s + 1] = best[s, :, g * STRIDE : (g + 1) * STRIDE]
    for g in range(1, CHUNKS):
        pltpu.make_async_remote_copy(
            src_ref=back_out.at[g], dst_ref=back_mid.at[g],
            send_sem=back_sent_sem.at[0], recv_sem=back_got_sem.at[0],
            device_id=column(g, -1) + far[0], device_id_type=LOGICAL,
        ).start()
    back_mid[0] = back_out[0]
    rest = pl.ds(1, CHUNKS - 1)
    pltpu.make_async_copy(back_mid.at[rest], back_mid.at[rest], back_got_sem.at[0]).wait()
    lane = iota((CHUNKS, 128), 1)
    first, second = back_mid[:, 0, :], back_mid[:, 1, :]
    back_half[0] = jnp.where(lane < HALF, first, pltpu.roll(second, HALF, 1))
    back_half[1] = jnp.where(lane < HALF, pltpu.roll(first, 128 - HALF, 1), second)
    for j in range(1, GROUP):
        pltpu.make_async_remote_copy(
            src_ref=back_half.at[j // NZ], dst_ref=back_in.at[j],
            send_sem=back_sent_sem.at[1], recv_sem=back_got_sem.at[1],
            device_id=here + far[j], device_id_type=LOGICAL,
        ).start()
    back_in[0] = back_half[0]
    rest = pl.ds(1, GROUP - 1)
    pltpu.make_async_copy(back_in.at[rest], back_in.at[rest], back_got_sem.at[1]).wait()

    at_row, at_lane = iota((16, 128), 0), iota((16, 128), 1)
    by_rank = ones_at(
        (at_lane < OWN * HALF) & (at_row == at_lane // HALF * 8 + at_lane % HALF % CAP)
    )
    values = jnp.where(wanted[...] > 0.5, back_in[...].reshape(N_DEV, 128), 0.0)
    hi, mid, lo = split3(values)
    answers = dot_t(by_rank, hi) + dot_t(by_rank, mid) + dot_t(by_rank, lo)
    hi, mid, lo = split3(answers)
    spread = dot(hi, pick[...]) + dot(mid, pick[...]) + dot(lo, pick[...])
    row = (ids_ref[...] & 1) * 8 + rank[...]
    out_ref[...] = jnp.sum(
        jnp.where(iota((16, ROWS), 0) == row, spread, 0.0), axis=0, keepdims=True
    )

    others = pl.ds(0, N_DEV - 1)
    pltpu.make_async_copy(send.at[others], send.at[others], sent_sem).wait()
    pltpu.make_async_copy(back_out.at[rest], back_out.at[rest], back_sent_sem.at[0]).wait()
    pltpu.make_async_copy(back_in.at[rest], back_in.at[rest], back_sent_sem.at[1]).wait()


def fast_kernel(
    ids_ref, embeds_hbm, out_ref, over_ref,
    embeds, send, recv, spill_out, spill_in, tag_out, tag_in, extra_out, extra_in,
    unit, bias, best, best_rows, rank, pick, undirect, unextra, tri, wanted,
    back_out, back_mid, back_half, back_in,
    load_sem, sent_sem, got_sem, in_sem, spill_sem, tag_sem, extra_sent_sem, extra_sem,
    back_sent_sem, back_got_sem,
):
    my_y = lax.axis_index("grp")
    my_dev = lax.axis_index("dev")
    my_x = my_dev // (NZ * NC)
    my_z = (my_dev // NC) % NZ
    my_c = my_dev % NC

    load = pltpu.make_async_copy(embeds_hbm, embeds, load_sem)
    load.start()

    def plane(sign):
        return [
            (my_z + sign * (j % NZ) + NZ) % NZ * NC + (my_c + j // NZ) % NC for j in range(GROUP)
        ]

    def column(g, sign):
        y = (my_y + sign * (g // NX) + NY) % NY
        x = (my_x + sign * (g % NX) + NX) % NX
        return (y * NX + x) * (NZ * NC)

    near = plane(1)
    here = column(0, 1)

    barrier = pltpu.get_barrier_semaphore()
    for j in range(1, GROUP):
        pl.semaphore_signal(barrier, inc=1, device_id=here + near[j], device_id_type=LOGICAL)
    for g in range(1, CHUNKS):
        pl.semaphore_signal(
            barrier, inc=1, device_id=column(g, 1) + near[0], device_id_type=LOGICAL
        )

    tri[...] = ones_at(
        (iota((128, 256), 0) < iota((128, 256), 1)) | (iota((128, 256), 1) >= 128)
    )

    ids = ids_ref[...]
    owner = ids >> 1
    sub = ids & 1
    dy = ((owner >> 6) - my_y) & (NY - 1)
    dx = ((owner >> 4) - my_x) & (NX - 1)
    dz = ((owner >> 1) - my_z) & (NZ - 1)
    dc = (owner - my_c) & (NC - 1)
    chunk = dy * NX + dx
    member_of = dc * NZ + dz
    rank[...] = jnp.zeros((1, ROWS), jnp.int32)

    def count_before(key, kinds):
        member = iota((kinds, ROWS), 0) == key
        blocks = [slice(b * 128, (b + 1) * 128) for b in range(ROWS // 128)]
        flags = ones_at(member)
        sums = dot(jnp.concatenate([flags[:, b] for b in blocks], axis=0), tri[...])
        seen = jnp.zeros((kinds, 128), jnp.float32)
        before = []
        for n, b in enumerate(blocks):
            part = sums[n * kinds : (n + 1) * kinds]
            before.append(
                jnp.sum(
                    jnp.where(member[:, b], part[:, :128] + seen, 0.0), axis=0, keepdims=True
                )
            )
            seen = seen + part[:, 128:]
        return jnp.concatenate(before, axis=1).astype(jnp.int32), seen

    def rank_chunk(g):
        key = jnp.where(chunk == g, sub * GROUP + member_of, -1)
        rank[...] += count_before(key, OWN * GROUP)[0]

    def chosen_rows(place, amount):
        chosen = jnp.where(iota((amount, ROWS), 0) == place, 1.0, 0.0)
        rows = dot(chosen.astype(jnp.bfloat16), embeds[...])
        rows = rows * lax.rsqrt(jnp.sum(rows * rows, axis=1, keepdims=True) + 1e-06)
        return chosen, rows

    def mark_empty(rows, chosen):
        empty = jnp.sum(chosen, axis=1, keepdims=True) < 0.5
        return jnp.where((iota(rows.shape, 1) == 0) & empty, DEAD, rows)

    def make_direct(first, chunks):
        order = chunk - first
        mine = (order >= 0) & (order < chunks) & (rank[...] < DIRECT)
        slot = ((order * GROUP + member_of) * OWN + sub) * DIRECT + rank[...]
        chosen, rows = chosen_rows(jnp.where(mine, slot, -1), chunks * GROUP * OWN * DIRECT)
        rows = mark_empty(rows, chosen).reshape(chunks * GROUP, OWN * DIRECT, FEAT)
        block = jnp.concatenate([rows[:, :, : FEAT // 2], rows[:, :, FEAT // 2 :]], axis=1)
        send[pl.ds(first * GROUP, chunks * GROUP)] = block.astype(jnp.bfloat16)

    def send_chunk(g, first, sem):
        base = column(g, 1)
        for j in range(first, GROUP):
            k = g * GROUP + j
            pltpu.make_async_remote_copy(
                src_ref=send.at[k], dst_ref=recv.at[k], send_sem=sent_sem, recv_sem=got_sem.at[sem],
                device_id=base + near[j], device_id_type=LOGICAL,
            ).start()

    def rank_step(g, carry):
        rank_chunk(g)
        return carry

    def send_step(q, carry):
        make_direct(2 * q, 2)
        send_chunk(2 * q, 0, q)
        send_chunk(2 * q + 1, 0, q)
        return carry

    rank_chunk(0)
    rank_chunk(1)
    load.wait()
    make_direct(0, 2)
    pl.semaphore_wait(barrier, GROUP - 1 + CHUNKS - 1)
    for g in range(1, CHUNKS):
        pl.semaphore_signal(in_sem, inc=1, device_id=column(g, 1) + near[0], device_id_type=LOGICAL)
    send_chunk(0, 1, 0)
    pltpu.make_async_copy(send.at[0], recv.at[0], got_sem.at[0]).start()
    lax.fori_loop(2, MEANWHILE, rank_step, 0)
    pl.semaphore_wait(in_sem, CHUNKS - 1)
    send_chunk(1, 0, 0)
    lax.fori_loop(MEANWHILE, CHUNKS, rank_step, 0)

    beyond = rank[...] >= DIRECT
    spot, totals = count_before(jnp.where(beyond, dz, -1), 2 * NZ)
    over = jnp.max(totals, axis=(0, 1), keepdims=True) > SPILL
    over = jnp.where(over, 1.0, 0.0)
    place = jnp.where(beyond & (spot < SPILL), dz * SPILL + spot, -1)
    chosen, rows = chosen_rows(place, NZ * SPILL)
    spill_out[...] = rows.astype(jnp.bfloat16).reshape(NZ, SPILL, FEAT)
    spill_in[0] = rows[:SPILL].astype(jnp.bfloat16)
    label = ((chunk * NC + dc) * OWN + sub) * EXTRA + rank[...] - DIRECT + 1
    labels = jnp.sum(jnp.where(chosen > 0.5, label.astype(jnp.float32), 0.0), axis=1, keepdims=True)
    same = iota((LANES, LANES), 0) == iota((LANES, LANES), 1)
    for b in range(NZ * SPILL // LANES):
        part = labels[b * LANES : (b + 1) * LANES]
        line = jnp.sum(jnp.where(same, part, 0.0), axis=0, keepdims=True)
        tag_out[2 * b] = line.astype(jnp.int32)
        tag_out[2 * b + 1] = pltpu.roll(line, SPILL, 1).astype(jnp.int32)
    tag_in[0] = tag_out[0]
    for piece in range(SPILL // MSG_R):
        for d in Z_ORDER:
            rows = pl.ds(piece * MSG_R, MSG_R)
            pltpu.make_async_remote_copy(
                src_ref=spill_out.at[d, rows], dst_ref=spill_in.at[d, rows],
                send_sem=spill_sem.at[0], recv_sem=spill_sem.at[1],
                device_id=here + near[d], device_id_type=LOGICAL,
            ).start()
            if piece == 0:
                pltpu.make_async_remote_copy(
                    src_ref=tag_out.at[d], dst_ref=tag_in.at[d],
                    send_sem=tag_sem.at[0], recv_sem=tag_sem.at[1],
                    device_id=here + near[d], device_id_type=LOGICAL,
                ).start()

    lax.fori_loop(EARLY, AHEAD, send_step, 0)

    others = pl.ds(1, NZ - 1)
    pltpu.make_async_copy(spill_in.at[others], spill_in.at[others], spill_sem.at[1]).wait()
    pltpu.make_async_copy(tag_in.at[others], tag_in.at[others], tag_sem.at[1]).wait()
    lane = iota((1, LANES), 1)
    onward = []
    for b in range(NZ // 2):
        line = jnp.where(lane < SPILL, tag_in[2 * b], pltpu.roll(tag_in[2 * b + 1], SPILL, 1))
        at = line - 1
        at = (at >> 2) * (NZ * OWN * EXTRA) + (2 * b + (lane >> 6)) * (OWN * EXTRA) + (at & 3)
        onward.append(jnp.where(line > 0, at, -1))
    onward = jnp.concatenate(onward, axis=1)

    def onward_step(e, carry):
        amount = E_OWN * NZ * OWN * EXTRA
        chosen = jnp.where(iota((amount, NZ * SPILL), 0) + e * amount == onward, 1.0, 0.0)
        rows = dot(chosen.astype(jnp.bfloat16), spill_in[...].reshape(NZ * SPILL, FEAT))
        rows = mark_empty(rows, chosen).astype(jnp.bfloat16)
        extra_out[pl.ds(e * E_OWN, E_OWN)] = rows.reshape(E_OWN, NZ * OWN * EXTRA, FEAT)
        return carry

    lax.fori_loop(0, E_STEPS, onward_step, 0)
    pltpu.make_async_copy(extra_out.at[0], extra_in.at[0], extra_sem.at[0]).start()
    for j in range(E_OWN):
        for e in (1, 3, 2, 0):
            k = e * E_OWN + j
            if k > 0:
                pltpu.make_async_remote_copy(
                    src_ref=extra_out.at[k], dst_ref=extra_in.at[k],
                    send_sem=extra_sent_sem, recv_sem=extra_sem.at[e],
                    device_id=column(k // NC, 1) + near[j % NC * NZ], device_id_type=LOGICAL,
                ).start()

    lax.fori_loop(AHEAD, D_STEPS, send_step, 0)

    for s in range(OWN):
        unit[s] = jnp.zeros((WIDTH, FEAT), jnp.bfloat16)
        bias[s] = jnp.full((1, WIDTH), FAR, jnp.float32)
        best[s] = jnp.full((1, WIDTH), -1.0, jnp.float32)
    to, frm = iota((OWN * LANES, PAIR * MSG_R), 0), iota((OWN * LANES, PAIR * MSG_R), 1)
    slot = to % LANES
    at = slot // DIRECT * MSG_R + to // LANES * DIRECT + slot % DIRECT
    undirect[0] = ones_at(frm == at)
    undirect[1] = ones_at(frm == at + OWN * DIRECT)
    to, frm = iota((OWN * LANES, OWN * LANES), 0), iota((OWN * LANES, OWN * LANES), 1)
    slot = to % LANES
    unextra[...] = ones_at(
        frm == slot // EXTRA * (OWN * EXTRA) + to // LANES * EXTRA + slot % EXTRA
    )
    pick[...] = ones_at(iota((N_DEV, ROWS), 0) == member_of * CHUNKS + chunk)
    lane = iota((N_DEV, LANES), 1)
    lane_dz = jnp.where(lane < 64, lane % 32 // DIRECT, lane % 16 // EXTRA)
    wanted[...] = jnp.where(
        (lane_dz == (iota((N_DEV, LANES), 0) // CHUNKS) % NZ) & (lane < 96), 1.0, 0.0
    )

    def compare(t, both):
        at = pl.ds(pl.multiple_of(t * LANES, LANES), LANES)
        for s in range(OWN):
            part = both[s * LANES : (s + 1) * LANES]
            new = part.astype(jnp.bfloat16)
            new_bias = jnp.where(part[:, :1] > 2.0, FAR, 0.0)
            same = iota((LANES, LANES), 0) == iota((LANES, LANES), 1)
            new_row = jnp.sum(jnp.where(same, new_bias, 0.0), axis=0, keepdims=True)
            sims = dot_t(new, unit[s])
            by_new = jnp.max(sims + new_bias, axis=0, keepdims=True)
            by_old = jnp.full((LANES, LANES), -1.0, jnp.float32)
            for h in range(D_STEPS + E_STEPS):
                lanes = slice(h * LANES, (h + 1) * LANES)
                by_old = jnp.maximum(by_old, sims[:, lanes] + bias[s, :, lanes])
            by_old = jnp.max(by_old.T, axis=0, keepdims=True)
            among = jnp.where(same, -1.0, dot_t(new, new) + new_bias)
            best[s] = jnp.maximum(best[s], jnp.where(bias[s] > -1.0, by_new, -1.0))
            best[s, :, at] = jnp.maximum(
                jnp.maximum(by_old, jnp.max(among, axis=0, keepdims=True)), -1.0
            )
            unit[s, at] = new
            bias[s, :, at] = new_row

    def direct_step(q, carry):
        mine = pl.ds(q * PAIR, PAIR)
        pltpu.make_async_copy(recv.at[mine], recv.at[mine], got_sem.at[q]).wait()
        block = recv[mine].reshape(PAIR * MSG_R, FEAT // 2)
        compare(q, jnp.concatenate([dot(undirect[0], block), dot(undirect[1], block)], axis=1))
        return carry

    def extra_step(e, carry):
        mine = pl.ds(e * E_OWN, E_OWN)
        pltpu.make_async_copy(extra_in.at[mine], extra_in.at[mine], extra_sem.at[e]).wait()
        block = extra_in[mine].reshape(OWN * LANES, FEAT)
        compare(D_STEPS + e, dot(unextra[...], block))
        return carry

    lax.fori_loop(0, BEFORE, direct_step, 0)
    lax.fori_loop(0, E_STEPS, extra_step, 0)
    lax.fori_loop(BEFORE, D_STEPS, direct_step, 0)

    far = plane(-1)
    for s in range(OWN):
        for t in range(D_STEPS + E_STEPS):
            best_rows[s, t : t + 1] = best[s, :, t * LANES : (t + 1) * LANES]
    lane = iota((D_STEPS, LANES), 1)
    first, second = best_rows[0, :D_STEPS], best_rows[1, :D_STEPS]
    even = jnp.where(lane < 64, first, pltpu.roll(second, 64, 1))
    odd = jnp.where(lane < 64, pltpu.roll(first, 64, 1), second)
    for q in range(D_STEPS):
        back_out[2 * q, 0:1] = even[q : q + 1]
        back_out[2 * q + 1, 0:1] = odd[q : q + 1]
    first, second = best_rows[0, D_STEPS:], best_rows[1, D_STEPS:]
    for r in range(4):
        line = jnp.where(
            lane < 32,
            first if r == 0 else pltpu.roll(first, 128 - 32 * r, 1),
            second if r == 1 else pltpu.roll(second, (160 - 32 * r) % 128, 1),
        )
        line = jnp.where(lane < 96, line, over)
        for e in range(E_STEPS):
            back_out[4 * e + r, 1:2] = line[e : e + 1]
    for g in range(1, CHUNKS):
        pltpu.make_async_remote_copy(
            src_ref=back_out.at[g], dst_ref=back_mid.at[g],
            send_sem=back_sent_sem.at[0], recv_sem=back_got_sem.at[0],
            device_id=column(g, -1) + far[0], device_id_type=LOGICAL,
        ).start()
    back_mid[0] = back_out[0]
    rest = pl.ds(1, CHUNKS - 1)
    pltpu.make_async_copy(back_mid.at[rest], back_mid.at[rest], back_got_sem.at[0]).wait()
    lane = iota((CHUNKS, LANES), 1)
    main, more = back_mid[:, 0, :], back_mid[:, 1, :]
    over = jnp.max(jnp.where(lane < 96, 0.0, more), axis=(0, 1), keepdims=True)
    for h in range(NC):
        line = jnp.where(lane < 96, pltpu.roll(more, 48 - 16 * h, 1), over)
        line = jnp.where(lane < 80, pltpu.roll(more, 64 - 16 * h, 1), line)
        line = jnp.where(lane < 64, pltpu.roll(main, 96 - 32 * h, 1), line)
        back_half[h] = jnp.where(lane < 32, main if h == 0 else pltpu.roll(main, 96, 1), line)
    for j in range(1, GROUP):
        pltpu.make_async_remote_copy(
            src_ref=back_half.at[j // NZ], dst_ref=back_in.at[j],
            send_sem=back_sent_sem.at[1], recv_sem=back_got_sem.at[1],
            device_id=here + far[j], device_id_type=LOGICAL,
        ).start()
    back_in[0] = back_half[0]
    rest = pl.ds(1, GROUP - 1)
    pltpu.make_async_copy(back_in.at[rest], back_in.at[rest], back_got_sem.at[1]).wait()

    at_row, lane = iota((16, LANES), 0), iota((16, LANES), 1)
    kind = jnp.where(
        lane < 64, lane // 32 * 8 + lane % DIRECT, (lane - 64) // 16 * 8 + DIRECT + lane % EXTRA
    )
    by_rank = ones_at((lane < 96) & (at_row == kind))
    everything = back_in[...].reshape(N_DEV, LANES)
    values = jnp.where(wanted[...] > 0.5, everything, 0.0)
    hi, mid, lo = split3(values)
    answers = dot_t(by_rank, hi) + dot_t(by_rank, mid) + dot_t(by_rank, lo)
    hi, mid, lo = split3(answers)
    spread = dot(hi, pick[...]) + dot(mid, pick[...]) + dot(lo, pick[...])
    row = (ids_ref[...] & 1) * 8 + rank[...]
    out_ref[...] = jnp.sum(
        jnp.where(iota((16, ROWS), 0) == row, spread, 0.0), axis=0, keepdims=True
    )
    lane = iota((N_DEV, LANES), 1)
    over = jnp.max(jnp.where(lane < 96, 0.0, everything), axis=(0, 1), keepdims=True)
    over_ref[...] = jnp.broadcast_to(over, (1, LANES))

    peers = pl.ds(1, N_DEV - 1)
    pltpu.make_async_copy(send.at[peers], send.at[peers], sent_sem).wait()
    pltpu.make_async_copy(spill_out.at[others], spill_out.at[others], spill_sem.at[0]).wait()
    pltpu.make_async_copy(tag_out.at[others], tag_out.at[others], tag_sem.at[0]).wait()
    peers = pl.ds(1, OWNERS - 1)
    pltpu.make_async_copy(extra_out.at[peers], extra_out.at[peers], extra_sent_sem).wait()
    pltpu.make_async_copy(back_out.at[rest], back_out.at[rest], back_sent_sem.at[0]).wait()
    pltpu.make_async_copy(back_in.at[rest], back_in.at[rest], back_sent_sem.at[1]).wait()


def fast_nearest(ids, embeds):
    bf16, f32, i32 = jnp.bfloat16, jnp.float32, jnp.int32
    return pl.pallas_call(
        fast_kernel,
        out_shape=(
            jax.ShapeDtypeStruct((1, ROWS), f32),
            jax.ShapeDtypeStruct((1, LANES), f32),
        ),
        in_specs=[
            pl.BlockSpec(memory_space=pltpu.VMEM),
            pl.BlockSpec(memory_space=pl.ANY),
        ],
        out_specs=(
            pl.BlockSpec(memory_space=pltpu.VMEM),
            pl.BlockSpec(memory_space=pltpu.VMEM),
        ),
        scratch_shapes=[
            pltpu.VMEM((ROWS, FEAT), bf16),
            pltpu.VMEM((N_DEV, MSG_R, FEAT // 2), bf16),
            pltpu.VMEM((N_DEV, MSG_R, FEAT // 2), bf16),
            pltpu.VMEM((NZ, SPILL, FEAT), bf16),
            pltpu.VMEM((NZ, SPILL, FEAT), bf16),
            pltpu.VMEM((NZ, 1, LANES), i32),
            pltpu.VMEM((NZ, 1, LANES), i32),
            pltpu.VMEM((OWNERS, NZ * OWN * EXTRA, FEAT), bf16),
            pltpu.VMEM((OWNERS, NZ * OWN * EXTRA, FEAT), bf16),
            pltpu.VMEM((OWN, WIDTH, FEAT), bf16),
            pltpu.VMEM((OWN, 1, WIDTH), f32),
            pltpu.VMEM((OWN, 1, WIDTH), f32),
            pltpu.VMEM((OWN, 2 * D_STEPS, LANES), f32),
            pltpu.VMEM((1, ROWS), i32),
            pltpu.VMEM((N_DEV, ROWS), bf16),
            pltpu.VMEM((2, OWN * LANES, PAIR * MSG_R), bf16),
            pltpu.VMEM((OWN * LANES, OWN * LANES), bf16),
            pltpu.VMEM((128, 256), bf16),
            pltpu.VMEM((N_DEV, LANES), f32),
            pltpu.VMEM((CHUNKS, OWN, LANES), f32),
            pltpu.VMEM((CHUNKS, OWN, LANES), f32),
            pltpu.VMEM((NC, CHUNKS, LANES), f32),
            pltpu.VMEM((GROUP, CHUNKS, LANES), f32),
            pltpu.SemaphoreType.DMA,
            pltpu.SemaphoreType.DMA,
            pltpu.SemaphoreType.DMA((D_STEPS,)),
            pltpu.SemaphoreType.REGULAR,
            pltpu.SemaphoreType.DMA((2,)),
            pltpu.SemaphoreType.DMA((2,)),
            pltpu.SemaphoreType.DMA,
            pltpu.SemaphoreType.DMA((E_STEPS,)),
            pltpu.SemaphoreType.DMA((2,)),
            pltpu.SemaphoreType.DMA((2,)),
        ],
        compiler_params=pltpu.CompilerParams(
            collective_id=1, has_side_effects=True, vmem_limit_bytes=48 * 1024 * 1024
        ),
    )(ids, embeds)


def padded_nearest(ids, embeds):
    return pl.pallas_call(
        padded_kernel,
        out_shape=jax.ShapeDtypeStruct((1, ROWS), jnp.float32),
        in_specs=[
            pl.BlockSpec(memory_space=pltpu.VMEM),
            pl.BlockSpec(memory_space=pl.ANY),
        ],
        out_specs=pl.BlockSpec(memory_space=pltpu.VMEM),
        scratch_shapes=[
            pltpu.VMEM((ROWS, FEAT), jnp.bfloat16),
            pltpu.VMEM((N_DEV, MSG_R, MSG_C), jnp.bfloat16),
            pltpu.VMEM((N_DEV, MSG_R, MSG_C), jnp.bfloat16),
            pltpu.VMEM((OWN, CHUNKS * STRIDE, FEAT), jnp.bfloat16),
            pltpu.VMEM((OWN, 1, CHUNKS * STRIDE), jnp.float32),
            pltpu.VMEM((OWN, 1, CHUNKS * STRIDE), jnp.float32),
            pltpu.VMEM((1, ROWS), jnp.int32),
            pltpu.VMEM((N_DEV, ROWS), jnp.bfloat16),
            pltpu.VMEM((4, GROUP * MSG_R, OWN * SLOTS), jnp.bfloat16),
            pltpu.VMEM((4, OWN * STRIDE, GROUP * MSG_R), jnp.bfloat16),
            pltpu.VMEM((128, 256), jnp.bfloat16),
            pltpu.VMEM((N_DEV, 128), jnp.float32),
            pltpu.VMEM((CHUNKS, OWN, 128), jnp.float32),
            pltpu.VMEM((CHUNKS, OWN, 128), jnp.float32),
            pltpu.VMEM((NC, CHUNKS, 128), jnp.float32),
            pltpu.VMEM((GROUP, CHUNKS, 128), jnp.float32),
            pltpu.SemaphoreType.DMA,
            pltpu.SemaphoreType.DMA,
            pltpu.SemaphoreType.DMA((CHUNKS,)),
            pltpu.SemaphoreType.REGULAR,
            pltpu.SemaphoreType.DMA((2,)),
            pltpu.SemaphoreType.DMA((2,)),
        ],
        compiler_params=pltpu.CompilerParams(
            collective_id=0, has_side_effects=True, vmem_limit_bytes=48 * 1024 * 1024
        ),
    )(ids, embeds)


def on_device(embeds, cluster):
    ids = cluster.reshape(1, ROWS)
    nearest, over = fast_nearest(ids, embeds)
    nearest = lax.cond(
        over[0, 0] > 0.5, lambda: padded_nearest(ids, embeds), lambda: nearest
    )
    return nearest.reshape(ROWS)


def solution(mesh):
    return jax.shard_map(
        on_device,
        mesh=mesh,
        in_specs=(P(("grp", "dev"), None), P(("grp", "dev"), None)),
        out_specs=P(("grp", "dev")),
        check_vma=False,
    )
```
